768 devices in a mesh: dp: 48 (over z, y_hi, core), mp: 16 (over y_lo, x).
Axes of the slice: x: 4, y: 8 (y_hi: 2, y_lo: 4; y = y_hi * 4 + y_lo), z: 12, core: 2. Of those that a mesh axis runs over, the one named last changes fastest.
Arguments:
- hidden: bfloat16 [768, 64, 1152], P('dp', None, 'mp'), may hold values from -6 to 6
- counts: int32 [768], P('dp'), may hold values from 1 to 64, as said below
- w_qkv: bfloat16 [1152, 3456], P(None, 'mp')
- w_out: bfloat16 [1152, 1152], P('mp'), may hold values from -0.1875 to 0.1875
- images: float32 [768, 1152], P('dp'), may hold values from -0.1875 to 0.1875
- logit_params: float32 [2], replicated, may hold values from -0.5 to 2.5
Outputs:
- grad_qkv: float32 [1152, 3456], P('dp', 'mp')
- grad_out: float32 [1152, 1152], P('mp', 'dp')
The draws below stay inside these ranges and needn't reach their ends.
Inputs may be any that keep to these rules, and one draw needn't show every extreme that they name: `counts`: each caption has 1 to 64 real tokens; padding follows them.
All inputs are finite; a program needn't handle non-finite values.
Results may differ from the reference program's by a relative error of at most 0.012.
Values may be sent and summed in bfloat16 or wider, within the bound.
A program may use at most 32 MiB of HBM per device.

```python
import jax
import jax.numpy as jnp
from jax import lax

D = 1152
HEADS = 16
HD = 72
L = 64
CAPS = 16
CAPTIONS = 768


def draw_counts(key, part):
    key = jax.random.fold_in(key, 11)
    key_bucket, key_offset = jax.random.split(key)
    blocks = CAPTIONS // CAPS
    quarter = L // 4
    bucket = jax.random.randint(key_bucket, (blocks, 1), 0, 4)
    offset = jax.random.randint(key_offset, (blocks, CAPS), 1, quarter + 1)
    lengths = bucket * quarter + offset
    lengths = lengths.at[:, 0].set(L)
    return lengths.reshape(CAPTIONS).astype(jnp.int32)


def draw_w_qkv(key, part):
    key = jax.random.fold_in(key, 5)
    key_main = jax.random.fold_in(key, 0)
    weights = jax.random.normal(key_main, (D, HEADS, 3, HD), jnp.float32) / jnp.sqrt(jnp.float32(D))
    return weights.reshape(D, 3 * HEADS * HD).astype(jnp.bfloat16)


def shard_levels(rng, extent, cuts, smallest, top_value):
    def one(dim, parts):
        draws = jax.random.uniform(jax.random.fold_in(jax.random.fold_in(rng, 6), dim), (parts,), jnp.float32, smallest / len(cuts), top_value / len(cuts))
        return jnp.repeat(jnp.exp(draws), extent[dim] // parts).reshape((-1,) + (1,) * (len(extent) - dim - 1))

    level = one(*cuts[0])
    for cut in cuts[1:]:
        level = level * one(*cut)
    return level


def centred(stream_key, shape, scale, most, pieces=(), held_as=jnp.bfloat16):
    result = jax.random.normal(stream_key, shape, jnp.float32) * scale
    if len(pieces) > 0:
        result = shard_levels(stream_key, shape, pieces, -0.22, 0.18) * result
    return jnp.clip(result, min=-most, max=most).astype(held_as)


def setup_inputs(seed: int = 0) -> dict:
    seeds = jax.random.split(jax.random.key(seed), 7)
    return {
        "hidden": centred(seeds[0], (CAPTIONS, L, D), 1.0, 6.0, ((0, 48), (2, 16))),
        "counts": draw_counts(jax.random.fold_in(seeds[6], 71), 0),
        "w_qkv": draw_w_qkv(jax.random.fold_in(seeds[6], 71), 0),
        "w_out": centred(seeds[3], (HEADS * HD, D), D ** -0.5, 0.1875, ((0, 16),)),
        "images": centred(seeds[4], (CAPTIONS, D), D ** -0.5, 0.1875, ((0, 48),), jnp.float32),
        "logit_params": jnp.clip(jax.random.uniform(seeds[5], (2,), jnp.float32, -0.5, 2.5), -0.5, 2.5),
    }


def layer_norm(tokens):
    values = tokens.astype(jnp.float32)
    center = lax.optimization_barrier(jnp.mean(values, axis=-1, keepdims=True))
    spread = lax.optimization_barrier(jnp.mean((values - center) ** 2, axis=-1, keepdims=True))
    return ((values - center) * lax.rsqrt(spread + 1e-06)).astype(jnp.bfloat16)

def forward(hid_block, count_block, w_qkv, w_out):
    n_caps = hid_block.shape[0]
    live_mask = jnp.arange(L, dtype=jnp.int32)[None, :] < count_block[:, None]
    live_float = live_mask.astype(jnp.float32)
    inv_count = 1.0 / count_block.astype(jnp.float32)
    normed = layer_norm(hid_block)
    packed = jnp.dot(normed.reshape(n_caps * L, D), w_qkv, preferred_element_type=jnp.float32)
    packed = packed.astype(jnp.bfloat16).reshape(n_caps, L, HEADS, 3, HD)
    query_f = packed[:, :, :, 0, :].astype(jnp.float32)
    key_f = packed[:, :, :, 1, :].astype(jnp.float32)
    value_f = packed[:, :, :, 2, :].astype(jnp.float32)
    scale_inv = 1.0 / jnp.sqrt(jnp.float32(HD))
    scores = jnp.einsum('clhe,cmhe->chlm', query_f, key_f, precision=lax.Precision.HIGHEST) * scale_inv
    key_live = live_mask[:, None, None, :]
    top = lax.optimization_barrier(jnp.max(jnp.where(key_live, scores, -jnp.inf), axis=-1, keepdims=True))
    expo = jnp.where(key_live, jnp.exp(scores - top), 0.0)
    attn_probs = expo / lax.optimization_barrier(jnp.sum(expo, axis=-1, keepdims=True))
    rounded = lax.optimization_barrier(attn_probs.astype(jnp.bfloat16))
    attn_out = jnp.einsum('chlm,cmhe->clhe', rounded.astype(jnp.float32), value_f, precision=lax.Precision.HIGHEST).astype(jnp.bfloat16)
    pooled_mix = lax.optimization_barrier(jnp.sum(attn_out.astype(jnp.float32) * live_float[:, :, None, None], axis=1))
    pooled_mix = pooled_mix.reshape(n_caps, HEADS * HD) * inv_count[:, None]
    pooled_hid = lax.optimization_barrier(jnp.sum(hid_block.astype(jnp.float32) * live_float[:, :, None], axis=1)) * inv_count[:, None]
    pooled = pooled_hid + jnp.dot(pooled_mix, w_out.astype(jnp.float32), precision=lax.Precision.HIGHEST)
    return (normed, query_f, key_f, value_f, attn_probs, pooled_mix, pooled, live_float, inv_count)

def reference(hidden, counts, w_qkv, w_out, images, logit_params):
    blocks = CAPTIONS // CAPS
    hid_blocks = hidden.reshape(blocks, CAPS, L, D)
    count_blocks = counts.reshape(blocks, CAPS)
    pooled = lax.map(lambda pair: forward(pair[0], pair[1], w_qkv, w_out)[6], (hid_blocks, count_blocks))
    pooled = pooled.reshape(CAPTIONS, D)
    inv_norm = lax.rsqrt(lax.optimization_barrier(jnp.sum(pooled * pooled, axis=-1, keepdims=True)) + 1e-06)
    text_emb = pooled * inv_norm
    logit_scale = jnp.exp(logit_params[0])
    logit_bias = logit_params[1]
    logits = logit_scale * jnp.dot(text_emb, images.T, precision=lax.Precision.HIGHEST) + logit_bias
    row_ids = jnp.arange(CAPTIONS, dtype=jnp.int32)
    labels = jnp.where(row_ids[:, None] == row_ids[None, :], 1.0, -1.0).astype(jnp.float32)
    pair_grad = -labels * jax.nn.sigmoid(-labels * logits)
    text_grad = logit_scale * jnp.dot(pair_grad, images, precision=lax.Precision.HIGHEST)
    along = lax.optimization_barrier(jnp.sum(text_emb * text_grad, axis=-1, keepdims=True))
    pooled_grad = (text_grad - text_emb * along) * inv_norm
    grad_blocks = pooled_grad.reshape(blocks, CAPS, D)
    out_f = w_out.astype(jnp.float32)
    scale_inv = 1.0 / jnp.sqrt(jnp.float32(HD))

    def backward(carry, items):
        hid_block, count_block, grad_block = items
        normed, query_f, key_f, value_f, attn_probs, pooled_mix, pooled_b, live_float, inv_count = forward(hid_block, count_block, w_qkv, w_out)
        grad_o = jnp.dot(pooled_mix.T, grad_block, precision=lax.Precision.HIGHEST)
        per_caption = jnp.dot(grad_block, out_f.T, precision=lax.Precision.HIGHEST) * inv_count[:, None]
        per_caption = per_caption.reshape(CAPS, HEADS, HD)
        upstream = live_float[:, :, None, None] * per_caption[:, None, :, :]
        prob_grad = jnp.einsum('clhe,cmhe->chlm', upstream, value_f, precision=lax.Precision.HIGHEST)
        value_grad = jnp.einsum('chlm,clhe->cmhe', attn_probs, upstream, precision=lax.Precision.HIGHEST)
        score_grad = attn_probs * (prob_grad - lax.optimization_barrier(jnp.sum(attn_probs * prob_grad, axis=-1, keepdims=True)))
        query_grad = jnp.einsum('chlm,cmhe->clhe', score_grad, key_f, precision=lax.Precision.HIGHEST) * scale_inv
        key_grad = jnp.einsum('chlm,clhe->cmhe', score_grad, query_f, precision=lax.Precision.HIGHEST) * scale_inv
        qkv_grad = jnp.stack([query_grad, key_grad, value_grad], axis=3).astype(jnp.bfloat16)
        qkv_grad = qkv_grad.reshape(CAPS * L, 3 * HEADS * HD)
        grad_q = jnp.dot(normed.reshape(CAPS * L, D).T, qkv_grad, preferred_element_type=jnp.float32)
        return ((carry[0] + grad_q, carry[1] + grad_o), None)
    start = (jnp.zeros((D, 3 * HEADS * HD), jnp.float32), jnp.zeros((HEADS * HD, D), jnp.float32))
    totals, unused = lax.scan(backward, start, (hid_blocks, count_blocks, grad_blocks))
    return (totals[0], totals[1])
```

```python
import jax
import jax.numpy as jnp
from jax import lax
from jax.experimental import pallas as pl
from jax.experimental.pallas import tpu as pltpu
from jax.sharding import PartitionSpec as P

D = 1152
HD = 72
L = 64
CAPS = 16
XN = 4
YN = 4
MP = XN * YN
SUB = 256
SUBS = CAPS * L // SUB
WIDE = 384
GO_AT = 256
OWN = 24
SLICES = D // 128

MESH = pl.DeviceIdType.MESH
F32 = jnp.float32
BF16 = jnp.bfloat16


def dot_nn(a, b):
    return lax.dot_general(a, b, (((1,), (0,)), ((), ())), preferred_element_type=F32)


def dot_nt(a, b):
    return lax.dot_general(a, b, (((1,), (1,)), ((), ())), preferred_element_type=F32)


def dot_tn(a, b):
    return lax.dot_general(a, b, (((0,), (0,)), ((), ())), preferred_element_type=F32)


def eye(n):
    rows = lax.broadcasted_iota(jnp.int32, (n, n), 0)
    cols = lax.broadcasted_iota(jnp.int32, (n, n), 1)
    return (rows == cols).astype(F32).astype(BF16)


def split_two(a):
    high = a.astype(BF16)
    return high, (a - high.astype(F32)).astype(BF16)


def make_kernel(zn):
    right_steps, left_steps = zn // 2, (zn - 1) // 2

    def kernel(
        hid, counts, w_qkv, w_out, images, params,
        gq_out, go_out,
        gat, nrm, wt, img, qt, kt, vt, vtok, prob, wl, live_sc,
        part, part_in, pooled_in, grad, sib_out, sib_in, z_out, z_in, acc, y_in,
        y_s, y_r, xr_s, xr_r, xl_s, xl_r, fr_s, fr_r, fl_s, fl_r,
        iy_s, iy_r, ir_s, ir_r, il_s, il_r, is_s, is_r,
        b1_s, b1_r, b2_s, b2_r, c1_s, c1_r, c2_s, c2_r, c3_s, c3_r,
    ):
        dp, mp = lax.axis_index("dp"), lax.axis_index("mp")
        core, yh, z = dp % 2, (dp // 2) % 2, dp // 4
        x, y = mp % XN, mp // XN
        sibling = (dp + 1 - 2 * core, mp)
        across = (dp + 2 - 4 * yh, mp)

        def at_z(step):
            return (z + zn + step) % zn

        def dev_z(step):
            return (at_z(step) * 4 + yh * 2 + core, mp)

        def slot(dx, dy):
            return ((y + YN + dy) % YN) * XN + (x + XN + dx) % XN

        def remote(src, dst, send, recv, device):
            return pltpu.make_async_remote_copy(
                src_ref=src, dst_ref=dst, send_sem=send, recv_sem=recv,
                device_id=device, device_id_type=MESH,
            )

        barrier = pltpu.get_barrier_semaphore()
        for step in range(1, MP):
            pl.semaphore_signal(barrier, inc=1, device_id=(dp, (mp + step) % MP), device_id_type=MESH)
        for step in range(1, zn):
            pl.semaphore_signal(barrier, inc=1, device_id=dev_z(step), device_id_type=MESH)
        pl.semaphore_signal(barrier, inc=1, device_id=sibling, device_id_type=MESH)
        pl.semaphore_signal(barrier, inc=1, device_id=across, device_id_type=MESH)

        eye_hd = eye(HD)
        for i in range(SUBS):
            gat[i // 2, mp, i % 2] = dot_nt(eye_hd, hid[i * SUB:(i + 1) * SUB, :]).astype(BF16)
        img[z, core, yh] = images[...].astype(BF16)

        pl.semaphore_wait(barrier, MP - 1 + zn - 1 + 2)

        def send_y(h, k):
            own = gat.at[h, mp]
            return remote(own, own, y_s.at[h, k - 1], y_r.at[h, k - 1], (dp, slot(0, k)))

        def recv_y(h, k):
            got = gat.at[h, slot(0, -k)]
            return remote(got, got, y_s.at[h, k - 1], y_r.at[h, k - 1], (dp, slot(0, k)))

        def send_xr(h, k):
            block = gat.at[h, slot(0, -k)]
            return remote(block, block, xr_s.at[h, k], xr_r.at[h, k], (dp, slot(1, 0)))

        def recv_xr(h, k):
            block = gat.at[h, slot(-1, -k)]
            return remote(block, block, xr_s.at[h, k], xr_r.at[h, k], (dp, slot(1, 0)))

        def send_xl(h, k):
            block = gat.at[h, slot(0, -k)]
            return remote(block, block, xl_s.at[h, k], xl_r.at[h, k], (dp, slot(-1, 0)))

        def recv_xl(h, k):
            block = gat.at[h, slot(1, -k)]
            return remote(block, block, xl_s.at[h, k], xl_r.at[h, k], (dp, slot(-1, 0)))

        def send_fr(h, k):
            block = gat.at[h, slot(-1, -k), 0]
            return remote(block, block, fr_s.at[h, k], fr_r.at[h, k], (dp, slot(1, 0)))

        def recv_fr(h, k):
            block = gat.at[h, slot(-2, -k), 0]
            return remote(block, block, fr_s.at[h, k], fr_r.at[h, k], (dp, slot(1, 0)))

        def send_fl(h, k):
            block = gat.at[h, slot(1, -k), 1]
            return remote(block, block, fl_s.at[h, k], fl_r.at[h, k], (dp, slot(-1, 0)))

        def recv_fl(h, k):
            block = gat.at[h, slot(2, -k), 1]
            return remote(block, block, fl_s.at[h, k], fl_r.at[h, k], (dp, slot(-1, 0)))

        def send_iy():
            own = img.at[z, core, yh]
            return remote(own, own, iy_s, iy_r, across)

        def recv_iy():
            got = img.at[z, core, 1 - yh]
            return remote(got, got, iy_s, iy_r, across)

        def send_ir(s):
            block = img.at[at_z(1 - s), core]
            return remote(block, block, ir_s.at[s - 1], ir_r.at[s - 1], dev_z(1))

        def recv_ir(s):
            block = img.at[at_z(-s), core]
            return remote(block, block, ir_s.at[s - 1], ir_r.at[s - 1], dev_z(1))

        def send_il(s):
            block = img.at[at_z(s - 1), core]
            return remote(block, block, il_s.at[s - 1], il_r.at[s - 1], dev_z(-1))

        def recv_il(s):
            block = img.at[at_z(s), core]
            return remote(block, block, il_s.at[s - 1], il_r.at[s - 1], dev_z(-1))

        def send_is(s):
            block = img.at[at_z(s), core]
            return remote(block, block, is_s.at[(s + zn) % zn], is_r.at[(s + zn) % zn], sibling)

        def recv_is(s):
            block = img.at[at_z(s), 1 - core]
            return remote(block, block, is_s.at[(s + zn) % zn], is_r.at[(s + zn) % zn], sibling)

        def image_step(s):
            if s == 1:
                recv_iy().wait_recv()
                send_is(0).start()
            elif s <= right_steps + 1:
                recv_ir(s - 1).wait_recv()
                if s - 1 <= left_steps:
                    recv_il(s - 1).wait_recv()
            if s <= right_steps:
                send_ir(s).start()
            if s <= left_steps:
                send_il(s).start()
            if s > 1:
                send_is(1 - s).start()
                if s - 1 <= left_steps:
                    send_is(s - 1).start()

        count_col = jnp.zeros((CAPS, 1), jnp.int32)
        row16 = lax.broadcasted_iota(jnp.int32, (CAPS, 1), 0)
        for c in range(CAPS):
            count_col = jnp.where(row16 == c, counts[c], count_col)
        inv_count = 1.0 / count_col.astype(F32)
        scale_inv = 1.0 / (float(HD) ** 0.5)

        for k in range(1, YN):
            send_y(0, k).start()
        send_xr(0, 0).start()
        send_xl(0, 0).start()
        send_iy().start()
        for k in range(1, YN):
            send_y(1, k).start()
        grad[...] = jnp.zeros_like(grad)
        eye_w = eye(3 * HD)
        for k in range(1, YN):
            recv_y(0, k).wait_recv()
            send_xr(0, k).start()
            send_xl(0, k).start()
        image_step(1)
        send_xr(1, 0).start()
        send_xl(1, 0).start()
        wt[...] = dot_nt(eye_w, w_qkv[...]).astype(BF16)
        for i in range(SUBS):
            caption = lax.broadcasted_iota(jnp.int32, (CAPS, SUB), 0)
            token = lax.broadcasted_iota(jnp.int32, (CAPS, SUB), 1) + (i * SUB)
            held = (token // L == caption) & (token % L < count_col)
            live_sc[i] = held.astype(F32)

        def forward_sub(h, s):
            i = h * 2 + s
            values = gat[h, :, s].astype(F32).reshape(D, SUB)
            center = jnp.sum(values, axis=0, keepdims=True) * (1.0 / D)
            values = values - center
            spread = jnp.sum(values * values, axis=0, keepdims=True) * (1.0 / D)
            normed = (values * lax.rsqrt(spread + 1e-06)).astype(BF16)
            nrm[i] = normed
            packed = dot_nn(wt[...], normed)
            q = packed[0:HD].astype(BF16)
            key = packed[HD:2 * HD].astype(BF16)
            val = packed[2 * HD:3 * HD].astype(BF16)
            qt[i] = q
            kt[i] = key
            vt[i] = val
            eye_s = eye(SUB)
            key_tok = dot_nt(eye_s, key).astype(BF16)
            vtok[i] = dot_nt(eye_s, val).astype(BF16)
            live_here = live_sc[i].astype(BF16)
            for b in range(SUB // 128):
                lanes = slice(b * 128, (b + 1) * 128)
                scores = dot_nn(key_tok[lanes], q[:, lanes]) * scale_inv
                first = (i * SUB + b * 128) // L
                s_row = lax.broadcasted_iota(jnp.int32, (128, 128), 0)
                t_col = lax.broadcasted_iota(jnp.int32, (128, 128), 1)
                limit = jnp.where(s_row < L, counts[first], counts[first + 1] + L)
                held = (s_row < limit) & (s_row // L == t_col // L)
                top = jnp.max(jnp.where(held, scores, -1e30), axis=0, keepdims=True)
                expo = jnp.where(held, jnp.exp(jnp.where(held, scores - top, 0.0)), 0.0)
                probs = expo / jnp.sum(expo, axis=0, keepdims=True)
                prob[i, b] = probs
                wl[i, :, lanes] = dot_nt(live_here[:, lanes], probs.astype(BF16))

        step = 2
        for k in range(YN):
            recv_xr(0, k).wait_recv()
            send_fr(0, k).start()
            recv_xl(0, k).wait_recv()
            send_fl(0, k).start()
            if k % 2 == 1:
                image_step(step)
                step += 1
        for k in range(1, YN):
            recv_y(1, k).wait_recv()
            send_xr(1, k).start()
            send_xl(1, k).start()
        for k in range(YN):
            recv_fr(0, k).wait_recv()
            recv_fl(0, k).wait_recv()
        if step <= right_steps + 1:
            image_step(step)
            step += 1
        forward_sub(0, 0)
        if step <= right_steps + 1:
            image_step(step)
            step += 1
        forward_sub(0, 1)
        for k in range(YN):
            recv_xr(1, k).wait_recv()
            send_fr(1, k).start()
            recv_xl(1, k).wait_recv()
            send_fl(1, k).start()
        while step <= right_steps + 1:
            image_step(step)
            step += 1
        for k in range(YN):
            recv_fr(1, k).wait_recv()
            recv_fl(1, k).wait_recv()
        forward_sub(1, 0)
        forward_sub(1, 1)

        mix = jnp.zeros((CAPS, HD), F32)
        hid_sum = jnp.zeros((CAPS, HD), F32)
        for i in range(SUBS):
            mix = mix + dot_nt(wl[i].astype(BF16), vt[i])
            hid_sum = hid_sum + dot_nn(live_sc[i].astype(BF16), hid[i * SUB:(i + 1) * SUB, :])
        mix = mix * inv_count
        hid_sum = hid_sum * inv_count
        place = (
            lax.broadcasted_iota(jnp.int32, (HD, D), 1)
            == lax.broadcasted_iota(jnp.int32, (HD, D), 0) + mp * HD
        ).astype(F32).astype(BF16)
        mix_hi, mix_lo = split_two(mix)
        hid_hi, hid_lo = split_two(hid_sum)
        w_rows = w_out[...]
        share = dot_nn(mix_hi, w_rows) + dot_nn(mix_lo, w_rows) + dot_nn(hid_hi, place) + dot_nn(hid_lo, place)
        for j in range(SLICES):
            part[j] = share[:, j * 128:(j + 1) * 128]

        def send_b1(j):
            return remote(part.at[j], part_in.at[mp], b1_s.at[j], b1_r.at[mp], (dp, j))

        def recv_b1(step):
            src = (mp + step) % MP
            return remote(part_in.at[src], part_in.at[src], b1_s.at[0], b1_r.at[src], (dp, mp))

        def send_b2(step):
            own = pooled_in.at[mp]
            return remote(own, own, b2_s.at[step - 1], b2_r.at[mp], (dp, (mp + step) % MP))

        def recv_b2(j):
            return remote(pooled_in.at[j], pooled_in.at[j], b2_s.at[0], b2_r.at[j], (dp, mp))

        for j in range(SLICES):
            @pl.when(mp != j)
            def _():
                send_b1(j).start()

        @pl.when(mp < SLICES)
        def _():
            total = part[mp]
            for step in range(1, MP):
                recv_b1(step).wait_recv()
                total = total + part_in[(mp + step) % MP]
            pooled_in[mp] = total
            for step in range(1, MP):
                send_b2(step).start()

        for s in range(1, zn):
            recv_is(s).wait_recv()
        recv_is(0).wait_recv()

        for j in range(SLICES):
            @pl.when(mp != j)
            def _():
                recv_b2(j).wait_recv()

        pooled = jnp.concatenate([pooled_in[j] for j in range(SLICES)], axis=1)
        inv_norm = lax.rsqrt(jnp.sum(pooled * pooled, axis=1, keepdims=True) + 1e-06)
        text_emb = pooled * inv_norm
        pictures = img[...].reshape(zn * 4 * CAPS, D)
        logit_scale = jnp.exp(jnp.full((CAPS, 1), params[0], F32))
        logits = logit_scale * dot_nt(text_emb.astype(BF16), pictures) + params[1]
        mine = ((z * 2 + core) * 2 + yh) * CAPS
        shape = (CAPS, zn * 4 * CAPS)
        same = lax.broadcasted_iota(jnp.int32, shape, 1) == lax.broadcasted_iota(jnp.int32, shape, 0) + mine
        label = jnp.where(same, 1.0, -1.0).astype(F32)
        pair_grad = -label * jax.nn.sigmoid(-label * logits)
        text_grad = logit_scale * dot_nn(pair_grad.astype(BF16), pictures)
        along = jnp.sum(text_emb * text_grad, axis=1, keepdims=True)
        pooled_grad = (text_grad - text_emb * along) * inv_norm
        grad[:, GO_AT:GO_AT + HD] = dot_tn(pooled_grad.astype(BF16), mix.astype(BF16))
        per_caption = dot_nt(w_rows, (pooled_grad * inv_count).astype(BF16)).astype(BF16)

        total = None
        for i in range(SUBS):
            pull = dot_nn(vtok[i], per_caption)
            owner = lax.broadcasted_iota(jnp.int32, (SUB, CAPS), 0) // L + (i * SUB // L)
            pull = jnp.sum(
                jnp.where(owner == lax.broadcasted_iota(jnp.int32, (SUB, CAPS), 1), pull, 0.0),
                axis=1, keepdims=True,
            )
            dq, dk = [], []
            for b in range(SUB // 128):
                lanes = slice(b * 128, (b + 1) * 128)
                first = (i * SUB + b * 128) // L
                t_row = lax.broadcasted_iota(jnp.int32, (1, 128), 1)
                limit = jnp.where(t_row < L, counts[first], counts[first + 1] + L)
                factor = jnp.where(t_row < limit, scale_inv, 0.0)
                probs = prob[i, b]
                here = pull[lanes]
                mean_pull = jnp.sum(probs * here, axis=0, keepdims=True)
                score_grad = (probs * (here - mean_pull) * factor).astype(BF16)
                dq.append(dot_nn(kt[i, :, lanes], score_grad))
                dk.append(dot_nt(qt[i, :, lanes], score_grad))
            dv = dot_nn(per_caption, wl[i].astype(BF16))
            qkv_grad = jnp.concatenate(
                [jnp.concatenate(dq, axis=1), jnp.concatenate(dk, axis=1), dv], axis=0
            ).astype(BF16)
            term = dot_nt(nrm[i], qkv_grad)
            total = term if total is None else total + term
        grad[:, 0:3 * HD] = total

        def hop(p):
            return (zn // 2 + ((p + 1) // 2) * (1 - 2 * (p % 2)) + zn) % zn

        def rows_of(step, which, half):
            first = at_z(step) * (4 * OWN) + half * (2 * OWN) + which * OWN
            return grad[pl.ds(pl.multiple_of(first, 8), OWN), :]

        def both(step, which):
            return jnp.concatenate([rows_of(step, which, 0), rows_of(step, which, 1)], axis=0)

        groups = 3
        per = zn // groups

        def send_c1(g):
            return remote(
                sib_out.at[pl.ds(g * per, per)], sib_in.at[pl.ds(g * per, per)],
                c1_s.at[g], c1_r.at[g], sibling,
            )

        def send_c2(p):
            return remote(z_out.at[p], z_in.at[p], c2_s.at[p], c2_r.at[p], dev_z(hop(p)))

        for g in range(groups):
            for p in range(g * per, (g + 1) * per):
                sib_out[p] = both(hop(p), 1 - core).astype(BF16)
            send_c1(g).start()
        for g in range(groups):
            send_c1(g).wait_recv()
            for p in range(g * per, (g + 1) * per):
                summed = both(hop(p), core) + sib_in[p].astype(F32)
                if p < zn - 1:
                    z_out[p] = summed.astype(BF16)
                    send_c2(p).start()
                else:
                    acc[...] = summed
        total = acc[...]
        for p in range(zn - 2, -1, -1):
            send_c2(p).wait_recv()
            total = total + z_in[p].astype(F32)
        acc[...] = total

        away = acc.at[pl.ds(pl.multiple_of((1 - yh) * OWN, 8), OWN)]
        last = remote(away, y_in, c3_s, c3_r, across)
        last.start()
        last.wait_recv()
        final = acc[pl.ds(pl.multiple_of(yh * OWN, 8), OWN), :] + y_in[...]
        gq_out[...] = final[:, 0:3 * HD]
        go_out[...] = final[:, GO_AT:GO_AT + HD]

        for h in range(2):
            for k in range(1, YN):
                send_y(h, k).wait_send()
            for k in range(YN):
                send_xr(h, k).wait_send()
                send_xl(h, k).wait_send()
                send_fr(h, k).wait_send()
                send_fl(h, k).wait_send()
        send_iy().wait_send()
        for s in range(1, right_steps + 1):
            send_ir(s).wait_send()
        for s in range(1, left_steps + 1):
            send_il(s).wait_send()
        for s in range(zn):
            send_is(s).wait_send()
        for j in range(SLICES):
            @pl.when(mp != j)
            def _():
                send_b1(j).wait_send()

        @pl.when(mp < SLICES)
        def _():
            for step in range(1, MP):
                send_b2(step).wait_send()

        for g in range(groups):
            send_c1(g).wait_send()
        for p in range(zn - 1):
            send_c2(p).wait_send()
        last.wait_send()

    return kernel


def solution(mesh):
    zn = mesh.shape["dp"] // 4
    dma = pltpu.SemaphoreType.DMA
    right_steps, left_steps = zn // 2, (zn - 1) // 2
    vmem = pl.BlockSpec(memory_space=pltpu.VMEM)
    smem = pl.BlockSpec(memory_space=pltpu.SMEM)

    def on_device(hidden, counts, w_qkv, w_out, images, logit_params):
        gq, go = pl.pallas_call(
            make_kernel(zn),
            out_shape=(
                jax.ShapeDtypeStruct((OWN, 3 * HD), F32),
                jax.ShapeDtypeStruct((OWN, HD), F32),
            ),
            in_specs=[vmem, smem, vmem, vmem, vmem, smem],
            out_specs=(vmem, vmem),
            scratch_shapes=[
                pltpu.VMEM((2, MP, 2, HD, SUB), BF16),
                pltpu.VMEM((SUBS, D, SUB), BF16),
                pltpu.VMEM((3 * HD, D), BF16),
                pltpu.VMEM((zn, 2, 2, CAPS, D), BF16),
                pltpu.VMEM((SUBS, HD, SUB), BF16),
                pltpu.VMEM((SUBS, HD, SUB), BF16),
                pltpu.VMEM((SUBS, HD, SUB), BF16),
                pltpu.VMEM((SUBS, SUB, HD), BF16),
                pltpu.VMEM((SUBS, SUB // 128, 128, 128), F32),
                pltpu.VMEM((SUBS, CAPS, SUB), F32),
                pltpu.VMEM((SUBS, CAPS, SUB), F32),
                pltpu.VMEM((SLICES, CAPS, 128), F32),
                pltpu.VMEM((MP, CAPS, 128), F32),
                pltpu.VMEM((SLICES, CAPS, 128), F32),
                pltpu.VMEM((D, WIDE), F32),
                pltpu.VMEM((zn, 2 * OWN, WIDE), BF16),
                pltpu.VMEM((zn, 2 * OWN, WIDE), BF16),
                pltpu.VMEM((zn - 1, 2 * OWN, WIDE), BF16),
                pltpu.VMEM((zn - 1, 2 * OWN, WIDE), BF16),
                pltpu.VMEM((2 * OWN, WIDE), F32),
                pltpu.VMEM((OWN, WIDE), F32),
                dma((2, YN - 1)), dma((2, YN - 1)),
                dma((2, YN)), dma((2, YN)), dma((2, YN)), dma((2, YN)),
                dma((2, YN)), dma((2, YN)), dma((2, YN)), dma((2, YN)),
                dma, dma,
                dma((right_steps,)), dma((right_steps,)), dma((left_steps,)), dma((left_steps,)),
                dma((zn,)), dma((zn,)),
                dma((SLICES,)), dma((MP,)), dma((MP - 1,)), dma((SLICES,)),
                dma((3,)), dma((3,)), dma((zn - 1,)), dma((zn - 1,)), dma, dma,
            ],
            compiler_params=pltpu.CompilerParams(
                collective_id=0, has_side_effects=True, vmem_limit_bytes=40 * 1024 * 1024
            ),
        )(hidden.reshape(CAPS * L, HD), counts, w_qkv, w_out, images, logit_params)
        return gq, go.T

    placed = (P("dp", None, "mp"), P("dp"), P(None, "mp"), P("mp", None), P("dp", None), P())
    return jax.shard_map(
        on_device,
        mesh=mesh,
        in_specs=placed,
        out_specs=(P("dp", "mp"), P("mp", "dp")),
        check_vma=False,
    )
```

```python
import jax
import jax.numpy as jnp
from jax import lax
from jax.experimental import pallas as pl
from jax.experimental.pallas import tpu as pltpu
from jax.sharding import PartitionSpec as P

D = 1152
HD = 72
L = 64
CAPS = 16
XN = 4
YN = 4
MP = XN * YN
SUB = 256
SUBS = CAPS * L // SUB
WIDE = 256
OWN = 24
ROWS = 32
GROUPS = 3
SLICES = D // 128

MESH = pl.DeviceIdType.MESH
F32 = jnp.float32
BF16 = jnp.bfloat16


def dot_nn(a, b):
    return lax.dot_general(a, b, (((1,), (0,)), ((), ())), preferred_element_type=F32)


def dot_nt(a, b):
    return lax.dot_general(a, b, (((1,), (1,)), ((), ())), preferred_element_type=F32)


def dot_tn(a, b):
    return lax.dot_general(a, b, (((0,), (0,)), ((), ())), preferred_element_type=F32)


def eye(n):
    rows = lax.broadcasted_iota(jnp.int32, (n, n), 0)
    cols = lax.broadcasted_iota(jnp.int32, (n, n), 1)
    return (rows == cols).astype(F32).astype(BF16)


def split_two(a):
    high = a.astype(BF16)
    return high, (a - high.astype(F32)).astype(BF16)


def make_kernel(zn):
    right_most, left_most = zn // 2, (zn - 1) // 2
    dests = 2 * zn
    per = dests // GROUPS

    def kernel(
        hid, counts, wt, w_out, images, params,
        gq_out, go_out,
        gat, nrm, img, qt, kt, vt, vtok, prob, wl, live_sc, share_hid,
        part, part_in, pooled_in, grad, outer, sib_out, sib_in, z_out, z_in, acc,
        y_s, y_r, yf_s, xr_s, xr_r, xl_s, xl_r, fr_s, fr_r, fl_s, fl_r,
        iy_s, iy_r, ir_s, ir_r, il_s, il_r, is_s, is_r,
        b1_s, b1_r, b2_s, b2_r, c1_s, c1_r, c2_s, c2_r,
    ):
        dp, mp = lax.axis_index("dp"), lax.axis_index("mp")
        core, yh, z = dp % 2, (dp // 2) % 2, dp // 4
        x, y = mp % XN, mp // XN
        sibling = (dp + 1 - 2 * core, mp)
        across = (dp + 2 - 4 * yh, mp)

        def at_z(step):
            return (z + zn + step) % zn

        def dev_z(step):
            return (at_z(step) * 4 + yh * 2 + core, mp)

        def hop(p):
            q = p // 2
            return (zn // 2 + ((q + 1) // 2) * (1 - 2 * (q % 2)) + zn) % zn

        def side(p):
            return yh if p % 2 == 1 else 1 - yh

        def dev_c(p):
            return (at_z(hop(p)) * 4 + side(p) * 2 + core, mp)

        def slot(dx, dy):
            return ((y + YN + dy) % YN) * XN + (x + XN + dx) % XN

        def remote(src, dst, send, recv, device):
            return pltpu.make_async_remote_copy(
                src_ref=src, dst_ref=dst, send_sem=send, recv_sem=recv,
                device_id=device, device_id_type=MESH,
            )

        barrier = pltpu.get_barrier_semaphore()
        for step in range(1, MP):
            pl.semaphore_signal(barrier, inc=1, device_id=(dp, (mp + step) % MP), device_id_type=MESH)
        for p in range(dests - 1):
            pl.semaphore_signal(barrier, inc=1, device_id=dev_c(p), device_id_type=MESH)
        pl.semaphore_signal(barrier, inc=1, device_id=sibling, device_id_type=MESH)

        eye_hd = eye(HD)
        for i in range(SUBS):
            gat[i // 2, mp, i % 2] = dot_nt(eye_hd, hid[i * SUB:(i + 1) * SUB, :]).astype(BF16)
        img[z, core, yh] = images[...].astype(BF16)

        count_col = jnp.zeros((CAPS, 1), jnp.int32)
        row16 = lax.broadcasted_iota(jnp.int32, (CAPS, 1), 0)
        for c in range(CAPS):
            count_col = jnp.where(row16 == c, counts[c], count_col)
        inv_count = 1.0 / count_col.astype(F32)
        scale_inv = 1.0 / (float(HD) ** 0.5)
        for i in range(SUBS):
            caption = lax.broadcasted_iota(jnp.int32, (CAPS, SUB), 0)
            token = lax.broadcasted_iota(jnp.int32, (CAPS, SUB), 1) + (i * SUB)
            held = (token // L == caption) & (token % L < count_col)
            live_sc[i] = held.astype(F32)
        hid_sum = jnp.zeros((CAPS, HD), F32)
        for i in range(SUBS):
            hid_sum = hid_sum + dot_nn(live_sc[i].astype(BF16), hid[i * SUB:(i + 1) * SUB, :])
        hid_hi, hid_lo = split_two(hid_sum * inv_count)
        place = (
            lax.broadcasted_iota(jnp.int32, (HD, D), 1)
            == lax.broadcasted_iota(jnp.int32, (HD, D), 0) + mp * HD
        ).astype(F32).astype(BF16)
        share_hid[...] = dot_nn(hid_hi, place) + dot_nn(hid_lo, place)
        grad[...] = jnp.zeros_like(grad)
        outer[...] = jnp.zeros_like(outer)

        pl.semaphore_wait(barrier, MP - 1 + dests - 1 + 1)

        def send_y(h, k):
            own = gat.at[h, mp]
            return remote(own, own, y_s.at[h, k - 1], y_r.at[h, k - 1], (dp, slot(0, k)))

        def recv_y(h, k):
            got = gat.at[h, slot(0, -k)]
            return remote(got, got, y_s.at[h, k - 1], y_r.at[h, k - 1], (dp, slot(0, k)))

        def forward_y(h, up):
            block = gat.at[h, slot(0, -2)]
            if up:
                return remote(block, block, yf_s.at[h], y_r.at[h, 2], (dp, slot(0, 1)))
            return remote(block, block, yf_s.at[h], y_r.at[h, 0], (dp, slot(0, -1)))

        def each_y(h, act):
            @pl.when(y != 3)
            def _():
                act(send_y(h, 1))

            act(send_y(h, 2))

            @pl.when(y != 0)
            def _():
                act(send_y(h, 3))

        def each_forward_y(h, act):
            @pl.when(y == 1)
            def _():
                act(forward_y(h, False))

            @pl.when(y == 2)
            def _():
                act(forward_y(h, True))

        k_near = 3 - 2 * (y % 2)
        k_far = 1 + (y + 1) // 2
        order = (0, k_near, 6 - k_near - k_far, k_far)

        def send_xr(h, k):
            block = gat.at[h, slot(0, -k)]
            return remote(block, block, xr_s.at[h, k], xr_r.at[h, k], (dp, slot(1, 0)))

        def recv_xr(h, k):
            block = gat.at[h, slot(-1, -k)]
            return remote(block, block, xr_s.at[h, k], xr_r.at[h, k], (dp, slot(1, 0)))

        def send_xl(h, k):
            block = gat.at[h, slot(0, -k)]
            return remote(block, block, xl_s.at[h, k], xl_r.at[h, k], (dp, slot(-1, 0)))

        def recv_xl(h, k):
            block = gat.at[h, slot(1, -k)]
            return remote(block, block, xl_s.at[h, k], xl_r.at[h, k], (dp, slot(-1, 0)))

        def send_fr(h, k):
            block = gat.at[h, slot(-1, -k), 0]
            return remote(block, block, fr_s.at[h, k], fr_r.at[h, k], (dp, slot(1, 0)))

        def recv_fr(h, k):
            block = gat.at[h, slot(-2, -k), 0]
            return remote(block, block, fr_s.at[h, k], fr_r.at[h, k], (dp, slot(1, 0)))

        def send_fl(h, k):
            block = gat.at[h, slot(1, -k), 1]
            return remote(block, block, fl_s.at[h, k], fl_r.at[h, k], (dp, slot(-1, 0)))

        def recv_fl(h, k):
            block = gat.at[h, slot(2, -k), 1]
            return remote(block, block, fl_s.at[h, k], fl_r.at[h, k], (dp, slot(-1, 0)))

        def line(q):
            return yh if q == 0 else 1 - yh

        def send_iy():
            own = img.at[z, core, yh]
            return remote(own, own, iy_s, iy_r, across)

        def recv_iy():
            got = img.at[z, core, 1 - yh]
            return remote(got, got, iy_s, iy_r, across)

        def send_ir(q, d):
            reach = 2 - d % 2
            block = img.at[at_z(reach - d), core, line(q)]
            return remote(block, block, ir_s.at[q, d - 1], ir_r.at[q, d - 1], dev_z(reach))

        def recv_ir(q, d):
            block = img.at[at_z(-d), core, line(q)]
            return remote(block, block, ir_s.at[q, d - 1], ir_r.at[q, d - 1], dev_z(1))

        def send_il(q, d):
            reach = 2 - d % 2
            block = img.at[at_z(d - reach), core, line(q)]
            return remote(block, block, il_s.at[q, d - 1], il_r.at[q, d - 1], dev_z(-reach))

        def recv_il(q, d):
            block = img.at[at_z(d), core, line(q)]
            return remote(block, block, il_s.at[q, d - 1], il_r.at[q, d - 1], dev_z(-1))

        def send_is(q, s):
            block = img.at[at_z(s), core, line(q)]
            n = (s + zn) % zn
            return remote(block, block, is_s.at[q, n], is_r.at[q, n], sibling)

        def recv_is(q, s):
            block = img.at[at_z(s), 1 - core, line(q)]
            n = (s + zn) % zn
            return remote(block, block, is_s.at[q, n], is_r.at[q, n], sibling)

        def image_step(q, step):
            near, far = 2 * step - 3, 2 * step - 2
            if step == 1:
                if q == 1:
                    recv_iy().wait_recv()
            else:
                for d in (far, near):
                    if d <= right_most:
                        recv_ir(q, d).wait_recv()
                    if d <= left_most:
                        recv_il(q, d).wait_recv()
                    if d == far and d + 1 <= right_most:
                        send_ir(q, d + 1).start()
                        if d + 2 <= right_most:
                            send_ir(q, d + 2).start()
                    if d == far and d + 1 <= left_most:
                        send_il(q, d + 1).start()
                        if d + 2 <= left_most:
                            send_il(q, d + 2).start()
                    if d <= right_most:
                        send_is(q, -d).start()
                    if d <= left_most:
                        send_is(q, d).start()
            if step == 1:
                for d in (2, 1):
                    send_ir(q, d).start()
                    send_il(q, d).start()
                send_is(q, 0).start()

        last_step = (right_most + 1) // 2 + 1

        each_y(0, lambda c: c.start())
        send_xr(0, 0).start()
        send_xl(0, 0).start()
        send_iy().start()
        image_step(0, 1)
        send_xr(1, 0).start()
        send_xl(1, 0).start()
        each_y(1, lambda c: c.start())

        def y_to_x(h, n):
            k = order[n]
            recv_y(h, k).wait_recv()
            if n == 3:
                each_forward_y(h, lambda c: c.start())
            send_xr(h, k).start()
            send_xl(h, k).start()

        def pass_on(h, n):
            k = order[n]
            recv_xr(h, k).wait_recv()
            send_fr(h, k).start()
            recv_xl(h, k).wait_recv()
            send_fl(h, k).start()

        def all_in(h):
            for k in range(YN):
                recv_fr(h, k).wait_recv()
                recv_fl(h, k).wait_recv()

        def forward_sub(h, s):
            i = h * 2 + s
            values = gat[h, :, s].astype(F32).reshape(D, SUB)
            center = jnp.sum(values, axis=0, keepdims=True) * (1.0 / D)
            values = values - center
            spread = jnp.sum(values * values, axis=0, keepdims=True) * (1.0 / D)
            normed = (values * lax.rsqrt(spread + 1e-06)).astype(BF16)
            nrm[i] = normed
            packed = dot_nn(wt[...], normed)
            q = packed[0:HD].astype(BF16)
            key = packed[HD:2 * HD].astype(BF16)
            val = packed[2 * HD:3 * HD].astype(BF16)
            qt[i] = q
            kt[i] = key
            vt[i] = val
            eye_s = eye(SUB)
            key_tok = dot_nt(eye_s, key).astype(BF16)
            vtok[i] = dot_nt(eye_s, val).astype(BF16)
            live_here = live_sc[i].astype(BF16)
            for b in range(SUB // 128):
                lanes = slice(b * 128, (b + 1) * 128)
                scores = dot_nn(key_tok[lanes], q[:, lanes]) * scale_inv
                first = (i * SUB + b * 128) // L
                s_row = lax.broadcasted_iota(jnp.int32, (128, 128), 0)
                t_col = lax.broadcasted_iota(jnp.int32, (128, 128), 1)
                limit = jnp.where(s_row < L, counts[first], counts[first + 1] + L)
                held = (s_row < limit) & (s_row // L == t_col // L)
                top = jnp.max(jnp.where(held, scores, -1e30), axis=0, keepdims=True)
                expo = jnp.where(held, jnp.exp(jnp.where(held, scores - top, 0.0)), 0.0)
                probs = expo / jnp.sum(expo, axis=0, keepdims=True)
                prob[i, b] = probs
                wl[i, :, lanes] = dot_nt(live_here[:, lanes], probs.astype(BF16))

        for n in range(1, YN):
            y_to_x(0, n)
        pass_on(0, 0)
        image_step(0, 2)
        y_to_x(1, 1)
        pass_on(0, 1)
        image_step(1, 1)
        y_to_x(1, 2)
        pass_on(0, 2)
        y_to_x(1, 3)
        pass_on(0, 3)
        image_step(0, 3)
        pass_on(1, 0)
        image_step(1, 2)
        pass_on(1, 1)
        for step in range(4, last_step + 1):
            image_step(0, step)
        pass_on(1, 2)
        pass_on(1, 3)
        all_in(0)
        forward_sub(0, 0)
        image_step(1, 3)
        forward_sub(0, 1)
        all_in(1)
        forward_sub(1, 0)
        forward_sub(1, 1)

        mix = jnp.zeros((CAPS, HD), F32)
        for i in range(SUBS):
            mix = mix + dot_nt(wl[i].astype(BF16), vt[i])
        mix = mix * inv_count
        mix_hi, mix_lo = split_two(mix)
        w_rows = w_out[...]
        share = dot_nn(mix_hi, w_rows) + dot_nn(mix_lo, w_rows) + share_hid[...]
        for j in range(SLICES):
            part[j] = share[:, j * 128:(j + 1) * 128]

        def send_b1(j):
            return remote(part.at[j], part_in.at[mp], b1_s.at[j], b1_r.at[mp], (dp, j))

        def recv_b1(step):
            src = (mp + step) % MP
            return remote(part_in.at[src], part_in.at[src], b1_s.at[0], b1_r.at[src], (dp, mp))

        def send_b2(step):
            own = pooled_in.at[mp]
            return remote(own, own, b2_s.at[step - 1], b2_r.at[mp], (dp, (mp + step) % MP))

        def recv_b2(j):
            return remote(pooled_in.at[j], pooled_in.at[j], b2_s.at[0], b2_r.at[j], (dp, mp))

        for j in range(SLICES):
            @pl.when(mp != j)
            def _():
                send_b1(j).start()

        for step in range(4, last_step + 1):
            image_step(1, step)

        @pl.when(mp < SLICES)
        def _():
            total = part[mp]
            for step in range(1, MP):
                recv_b1(step).wait_recv()
                total = total + part_in[(mp + step) % MP]
            pooled_in[mp] = total
            for step in range(1, MP):
                send_b2(step).start()

        for q in range(2):
            for s in range(zn):
                recv_is(q, s).wait_recv()

        for j in range(SLICES):
            @pl.when(mp != j)
            def _():
                recv_b2(j).wait_recv()

        pooled = jnp.concatenate([pooled_in[j] for j in range(SLICES)], axis=1)
        inv_norm = lax.rsqrt(jnp.sum(pooled * pooled, axis=1, keepdims=True) + 1e-06)
        text_emb = pooled * inv_norm
        pictures = img[...].reshape(zn * 4 * CAPS, D)
        logit_scale = jnp.exp(jnp.full((CAPS, 1), params[0], F32))
        logits = logit_scale * dot_nt(text_emb.astype(BF16), pictures) + params[1]
        mine = ((z * 2 + core) * 2 + yh) * CAPS
        shape = (CAPS, zn * 4 * CAPS)
        same = lax.broadcasted_iota(jnp.int32, shape, 1) == lax.broadcasted_iota(jnp.int32, shape, 0) + mine
        label = jnp.where(same, 1.0, -1.0).astype(F32)
        pair_grad = -label * jax.nn.sigmoid(-label * logits)
        text_grad = logit_scale * dot_nn(pair_grad.astype(BF16), pictures)
        along = jnp.sum(text_emb * text_grad, axis=1, keepdims=True)
        pooled_grad = (text_grad - text_emb * along) * inv_norm
        lane = lax.broadcasted_iota(jnp.int32, (HD, 3 * HD), 1)
        tile = (lane % HD == lax.broadcasted_iota(jnp.int32, (HD, 3 * HD), 0)).astype(F32).astype(BF16)
        mix_tiled = dot_nn(mix_hi, tile)
        grad_cols = dot_tn(pooled_grad.astype(BF16), eye(CAPS)).reshape(D // OWN, 3, 8, CAPS)
        lane = lax.broadcasted_iota(jnp.int32, (CAPS, 3 * HD), 1)
        total = None
        for b in range(3):
            term = dot_nn(
                grad_cols[:, b].reshape(D // 3, CAPS).astype(BF16),
                jnp.where(lane // HD == b, mix_tiled, 0.0).astype(BF16),
            )
            total = term if total is None else total + term
        outer[:, 0:3 * HD] = total
        per_caption = dot_nt(w_rows, (pooled_grad * inv_count).astype(BF16)).astype(BF16)

        grads = []
        for i in range(SUBS):
            pull = dot_nn(vtok[i], per_caption)
            owner = lax.broadcasted_iota(jnp.int32, (SUB, CAPS), 0) // L + (i * SUB // L)
            pull = jnp.sum(
                jnp.where(owner == lax.broadcasted_iota(jnp.int32, (SUB, CAPS), 1), pull, 0.0),
                axis=1, keepdims=True,
            )
            dq, dk = [], []
            for b in range(SUB // 128):
                lanes = slice(b * 128, (b + 1) * 128)
                first = (i * SUB + b * 128) // L
                t_row = lax.broadcasted_iota(jnp.int32, (1, 128), 1)
                limit = jnp.where(t_row < L, counts[first], counts[first + 1] + L)
                factor = jnp.where(t_row < limit, scale_inv, 0.0)
                probs = prob[i, b]
                here = pull[lanes]
                mean_pull = jnp.sum(probs * here, axis=0, keepdims=True)
                score_grad = (probs * (here - mean_pull) * factor).astype(BF16)
                dq.append(dot_nn(kt[i, :, lanes], score_grad))
                dk.append(dot_nt(qt[i, :, lanes], score_grad))
            dv = dot_nn(per_caption, wl[i].astype(BF16))
            qkv_grad = jnp.concatenate(
                [jnp.concatenate(dq, axis=1), jnp.concatenate(dk, axis=1), dv], axis=0
            ).astype(BF16)
            grads.append(qkv_grad)

        chips = per // 2

        def first_row(p):
            return at_z(hop(p)) * 4 + side(p) * 2

        def rows_of(p, which):
            inside = (p // 2 % chips) * (4 * OWN) + side(p) * (2 * OWN) + which * OWN
            return jnp.concatenate(
                [
                    grad[p // per, pl.ds(pl.multiple_of(inside, 8), OWN), :],
                    outer[pl.ds(pl.multiple_of((first_row(p) + which) * 8, 8), 8), :],
                ],
                axis=0,
            )

        def send_c1(g):
            return remote(
                sib_out.at[pl.ds(g * per, per)], sib_in.at[pl.ds(g * per, per)],
                c1_s.at[g], c1_r.at[g], sibling,
            )

        def send_c2(p):
            return remote(z_out.at[p], z_in.at[p], c2_s.at[p], c2_r.at[p], dev_c(p))

        def group_grad(g):
            total = None
            for i in range(SUBS):
                left = jnp.concatenate(
                    [
                        nrm[i, pl.ds(pl.multiple_of(at_z(hop(p)) * (4 * OWN), 32), 4 * OWN), :]
                        for p in range(g * per, (g + 1) * per, 2)
                    ],
                    axis=0,
                )
                term = dot_nt(left, grads[i])
                total = term if total is None else total + term
            grad[g, :, 0:3 * HD] = total
            for p in range(g * per, (g + 1) * per):
                sib_out[p] = rows_of(p, 1 - core).astype(BF16)
            send_c1(g).start()

        def group_send(g):
            send_c1(g).wait_recv()
            for p in range(g * per, (g + 1) * per):
                summed = rows_of(p, core) + sib_in[p].astype(F32)
                if p < dests - 1:
                    z_out[p] = summed.astype(BF16)
                    send_c2(p).start()
                else:
                    acc[...] = summed

        group_grad(0)
        for g in range(1, GROUPS):
            group_grad(g)
            group_send(g - 1)
        group_send(GROUPS - 1)
        total = acc[...]
        for p in range(dests - 1):
            send_c2(p).wait_recv()
            total = total + z_in[p].astype(F32)
        gq_out[...] = total[0:OWN, 0:3 * HD]
        go_out[...] = jnp.concatenate(
            [total[OWN:ROWS, b * HD:(b + 1) * HD] for b in range(3)], axis=0
        )

        for h in range(2):
            each_y(h, lambda c: c.wait_send())
            each_forward_y(h, lambda c: c.wait_send())
            for k in range(YN):
                send_xr(h, k).wait_send()
                send_xl(h, k).wait_send()
                send_fr(h, k).wait_send()
                send_fl(h, k).wait_send()
        send_iy().wait_send()
        for q in range(2):
            for d in range(1, right_most + 1):
                send_ir(q, d).wait_send()
            for d in range(1, left_most + 1):
                send_il(q, d).wait_send()
            for s in range(zn):
                send_is(q, s).wait_send()
        for j in range(SLICES):
            @pl.when(mp != j)
            def _():
                send_b1(j).wait_send()

        @pl.when(mp < SLICES)
        def _():
            for step in range(1, MP):
                send_b2(step).wait_send()

        for g in range(GROUPS):
            send_c1(g).wait_send()
        for p in range(dests - 1):
            send_c2(p).wait_send()

    return kernel


def solution(mesh):
    zn = mesh.shape["dp"] // 4
    dma = pltpu.SemaphoreType.DMA
    right_most, left_most = zn // 2, (zn - 1) // 2
    dests = 2 * zn
    vmem = pl.BlockSpec(memory_space=pltpu.VMEM)
    smem = pl.BlockSpec(memory_space=pltpu.SMEM)

    def on_device(hidden, counts, w_qkv, w_out, images, logit_params):
        gq, go = pl.pallas_call(
            make_kernel(zn),
            out_shape=(
                jax.ShapeDtypeStruct((OWN, 3 * HD), F32),
                jax.ShapeDtypeStruct((OWN, HD), F32),
            ),
            in_specs=[vmem, smem, vmem, vmem, vmem, smem],
            out_specs=(vmem, vmem),
            scratch_shapes=[
                pltpu.VMEM((2, MP, 2, HD, SUB), BF16),
                pltpu.VMEM((SUBS, D, SUB), BF16),
                pltpu.VMEM((zn, 2, 2, CAPS, D), BF16),
                pltpu.VMEM((SUBS, HD, SUB), BF16),
                pltpu.VMEM((SUBS, HD, SUB), BF16),
                pltpu.VMEM((SUBS, HD, SUB), BF16),
                pltpu.VMEM((SUBS, SUB, HD), BF16),
                pltpu.VMEM((SUBS, SUB // 128, 128, 128), F32),
                pltpu.VMEM((SUBS, CAPS, SUB), F32),
                pltpu.VMEM((SUBS, CAPS, SUB), F32),
                pltpu.VMEM((CAPS, D), F32),
                pltpu.VMEM((SLICES, CAPS, 128), F32),
                pltpu.VMEM((MP, CAPS, 128), F32),
                pltpu.VMEM((SLICES, CAPS, 128), F32),
                pltpu.VMEM((GROUPS, D // GROUPS, WIDE), F32),
                pltpu.VMEM((D // 3, WIDE), F32),
                pltpu.VMEM((dests, ROWS, WIDE), BF16),
                pltpu.VMEM((dests, ROWS, WIDE), BF16),
                pltpu.VMEM((dests - 1, ROWS, WIDE), BF16),
                pltpu.VMEM((dests - 1, ROWS, WIDE), BF16),
                pltpu.VMEM((ROWS, WIDE), F32),
                dma((2, YN - 1)), dma((2, YN - 1)), dma((2,)),
                dma((2, YN)), dma((2, YN)), dma((2, YN)), dma((2, YN)),
                dma((2, YN)), dma((2, YN)), dma((2, YN)), dma((2, YN)),
                dma, dma,
                dma((2, right_most)), dma((2, right_most)), dma((2, left_most)), dma((2, left_most)),
                dma((2, zn)), dma((2, zn)),
                dma((SLICES,)), dma((MP,)), dma((MP - 1,)), dma((SLICES,)),
                dma((GROUPS,)), dma((GROUPS,)), dma((dests - 1,)), dma((dests - 1,)),
            ],
            compiler_params=pltpu.CompilerParams(
                collective_id=0, has_side_effects=True, vmem_limit_bytes=40 * 1024 * 1024
            ),
        )(hidden.reshape(CAPS * L, HD), counts, w_qkv.T, w_out, images, logit_params)
        return gq, go.T

    placed = (P("dp", None, "mp"), P("dp"), P(None, "mp"), P("mp", None), P("dp", None), P())
    return jax.shard_map(
        on_device,
        mesh=mesh,
        in_specs=placed,
        out_specs=(P("dp", "mp"), P("mp", "dp")),
        check_vma=False,
    )
```

```python
import jax
import jax.numpy as jnp
from jax import lax
from jax.experimental import pallas as pl
from jax.experimental.pallas import tpu as pltpu
from jax.sharding import PartitionSpec as P

D = 1152
HD = 72
L = 64
CAPS = 16
XN = 4
YN = 4
MP = XN * YN
SUB = 256
SUBS = CAPS * L // SUB
WIDE = 256
OWN = 24
ROWS = 32
GROUPS = 3
SLICES = D // 128

MESH = pl.DeviceIdType.MESH
F32 = jnp.float32
BF16 = jnp.bfloat16


def dot_nn(a, b):
    return lax.dot_general(a, b, (((1,), (0,)), ((), ())), preferred_element_type=F32)


def dot_nt(a, b):
    return lax.dot_general(a, b, (((1,), (1,)), ((), ())), preferred_element_type=F32)


def dot_tn(a, b):
    return lax.dot_general(a, b, (((0,), (0,)), ((), ())), preferred_element_type=F32)


def eye(n):
    rows = lax.broadcasted_iota(jnp.int32, (n, n), 0)
    cols = lax.broadcasted_iota(jnp.int32, (n, n), 1)
    return (rows == cols).astype(F32).astype(BF16)


def split_two(a):
    high = a.astype(BF16)
    return high, (a - high.astype(F32)).astype(BF16)


def make_kernel(zn):
    right_most, left_most = zn // 2, (zn - 1) // 2
    dests = 2 * zn
    per = dests // GROUPS

    def kernel(
        hid, counts, wt, w_out, images, params,
        gq_out, go_out,
        gat, nrm, img, qt, kt, vt, vtok, prob, wl, live_sc, share_hid,
        part, part_in, pooled_in, grad, outer, sib_out, sib_in, z_out, z_in, acc,
        y_s, y_r, yf_s, xr_s, xr_r, xl_s, xl_r, fr_s, fr_r, fl_s, fl_r, yd_s, yd_r, x2_s, x2_r,
        iy_s, iy_r, ir_s, ir_r, il_s, il_r, is_s, is_r,
        b1_s, b1_r, b2_s, b2_r, c1_s, c1_r, c2_s, c2_r,
    ):
        dp, mp = lax.axis_index("dp"), lax.axis_index("mp")
        core, yh, z = dp % 2, (dp // 2) % 2, dp // 4
        x, y = mp % XN, mp // XN
        sibling = (dp + 1 - 2 * core, mp)
        across = (dp + 2 - 4 * yh, mp)

        def at_z(step):
            return (z + zn + step) % zn

        def dev_z(step):
            return (at_z(step) * 4 + yh * 2 + core, mp)

        def hop(p):
            q = p // 2
            return (zn // 2 + ((q + 1) // 2) * (1 - 2 * (q % 2)) + zn) % zn

        def side(p):
            return yh if p % 2 == 1 else 1 - yh

        def dev_c(p):
            return (at_z(hop(p)) * 4 + side(p) * 2 + core, mp)

        def slot(dx, dy):
            return ((y + YN + dy) % YN) * XN + (x + XN + dx) % XN

        def remote(src, dst, send, recv, device):
            return pltpu.make_async_remote_copy(
                src_ref=src, dst_ref=dst, send_sem=send, recv_sem=recv,
                device_id=device, device_id_type=MESH,
            )

        barrier = pltpu.get_barrier_semaphore()
        greeted = [sibling, across]
        greeted += [(dp, slot(0, k)) for k in range(1, YN)] + [(dp, slot(1, 0)), (dp, slot(-1, 0))]
        greeted += [dev_z(d) for d in (1, -1, 2, -2)]
        for device in greeted:
            pl.semaphore_signal(barrier, inc=1, device_id=device, device_id_type=MESH)

        eye_hd = eye(HD)
        for i in range(SUBS):
            gat[i // 2, mp, i % 2] = dot_nt(eye_hd, hid[i * SUB:(i + 1) * SUB, :]).astype(BF16)
        img[z, core, yh] = images[...].astype(BF16)

        pl.semaphore_wait(barrier, len(greeted))

        def send_y(h, k):
            own = gat.at[h, mp]
            return remote(own, own, y_s.at[h, k - 1], y_r.at[h, k - 1], (dp, slot(0, k)))

        def recv_y(h, k):
            got = gat.at[h, slot(0, -k)]
            return remote(got, got, y_s.at[h, k - 1], y_r.at[h, k - 1], (dp, slot(0, k)))

        def forward_y(h, up):
            block = gat.at[h, slot(0, -2)]
            if up:
                return remote(block, block, yf_s.at[h], y_r.at[h, 2], (dp, slot(0, 1)))
            return remote(block, block, yf_s.at[h], y_r.at[h, 0], (dp, slot(0, -1)))

        def each_y(h, act):
            @pl.when(y != 3)
            def _():
                act(send_y(h, 1))

            act(send_y(h, 2))

            @pl.when(y != 0)
            def _():
                act(send_y(h, 3))

        def each_forward_y(h, act):
            @pl.when(y == 1)
            def _():
                act(forward_y(h, False))

            @pl.when(y == 2)
            def _():
                act(forward_y(h, True))

        k_near = 3 - 2 * (y % 2)
        k_far = 1 + (y + 1) // 2
        order = (0, k_near, 6 - k_near - k_far, k_far)

        def send_xr(h, k):
            block = gat.at[h, slot(0, -k)]
            return remote(block, block, xr_s.at[h, k], xr_r.at[h, k], (dp, slot(1, 0)))

        def recv_xr(h, k):
            block = gat.at[h, slot(-1, -k)]
            return remote(block, block, xr_s.at[h, k], xr_r.at[h, k], (dp, slot(1, 0)))

        def send_xl(h, k):
            block = gat.at[h, slot(0, -k)]
            return remote(block, block, xl_s.at[h, k], xl_r.at[h, k], (dp, slot(-1, 0)))

        def recv_xl(h, k):
            block = gat.at[h, slot(1, -k)]
            return remote(block, block, xl_s.at[h, k], xl_r.at[h, k], (dp, slot(-1, 0)))

        def send_fr(h, k):
            block = gat.at[h, slot(-1, -k), 0]
            return remote(block, block, fr_s.at[h, k], fr_r.at[h, k], (dp, slot(1, 0)))

        def recv_fr(h, k):
            block = gat.at[h, slot(-2, -k), 0]
            return remote(block, block, fr_s.at[h, k], fr_r.at[h, k], (dp, slot(1, 0)))

        def send_fl(h, k):
            block = gat.at[h, slot(1, -k), 1]
            return remote(block, block, fl_s.at[h, k], fl_r.at[h, k], (dp, slot(-1, 0)))

        def recv_fl(h, k):
            block = gat.at[h, slot(2, -k), 1]
            return remote(block, block, fl_s.at[h, k], fl_r.at[h, k], (dp, slot(-1, 0)))

        def send_yd(k):
            block = gat.at[0, slot(2, 0)]
            return remote(block, block, yd_s.at[k - 1], yd_r.at[k - 1], (dp, slot(0, k)))

        def recv_yd(k):
            block = gat.at[0, slot(2, -k)]
            return remote(block, block, yd_s.at[k - 1], yd_r.at[k - 1], (dp, slot(0, k)))

        def send_x2():
            block = gat.at[1, slot(0, -k_far)]
            return remote(block, block, x2_s, x2_r, (dp, slot(2, 0)))

        def recv_x2():
            block = gat.at[1, slot(2, -k_far)]
            return remote(block, block, x2_s, x2_r, (dp, slot(2, 0)))

        def line(q):
            return yh if q == 0 else 1 - yh

        def send_iy():
            own = img.at[z, core, yh]
            return remote(own, own, iy_s, iy_r, across)

        def recv_iy():
            got = img.at[z, core, 1 - yh]
            return remote(got, got, iy_s, iy_r, across)

        def send_ir(q, d):
            reach = 2 - d % 2
            block = img.at[at_z(reach - d), core, line(q)]
            return remote(block, block, ir_s.at[q, d - 1], ir_r.at[q, d - 1], dev_z(reach))

        def recv_ir(q, d):
            block = img.at[at_z(-d), core, line(q)]
            return remote(block, block, ir_s.at[q, d - 1], ir_r.at[q, d - 1], dev_z(1))

        def send_il(q, d):
            reach = 2 - d % 2
            block = img.at[at_z(d - reach), core, line(q)]
            return remote(block, block, il_s.at[q, d - 1], il_r.at[q, d - 1], dev_z(-reach))

        def recv_il(q, d):
            block = img.at[at_z(d), core, line(q)]
            return remote(block, block, il_s.at[q, d - 1], il_r.at[q, d - 1], dev_z(-1))

        def send_is(q, s):
            block = img.at[at_z(s), core, line(q)]
            n = (s + zn) % zn
            return remote(block, block, is_s.at[q, n], is_r.at[q, n], sibling)

        def recv_is(q, s):
            block = img.at[at_z(s), 1 - core, line(q)]
            n = (s + zn) % zn
            return remote(block, block, is_s.at[q, n], is_r.at[q, n], sibling)

        def image_step(q, step):
            near, far = 2 * step - 3, 2 * step - 2
            if step == 1:
                if q == 1:
                    recv_iy().wait_recv()
            else:
                for d in (far, near):
                    if d <= right_most:
                        recv_ir(q, d).wait_recv()
                    if d <= left_most:
                        recv_il(q, d).wait_recv()
                    if d == far and d + 1 <= right_most:
                        send_ir(q, d + 1).start()
                        if d + 2 <= right_most:
                            send_ir(q, d + 2).start()
                    if d == far and d + 1 <= left_most:
                        send_il(q, d + 1).start()
                        if d + 2 <= left_most:
                            send_il(q, d + 2).start()
                    if d <= right_most:
                        send_is(q, -d).start()
                    if d <= left_most:
                        send_is(q, d).start()
            if step == 1:
                for d in (2, 1):
                    send_ir(q, d).start()
                    send_il(q, d).start()
                send_is(q, 0).start()

        last_step = (right_most + 1) // 2 + 1

        each_y(0, lambda c: c.start())
        send_xr(0, 0).start()
        send_xl(0, 0).start()
        send_iy().start()
        image_step(0, 1)
        send_xr(1, 0).start()
        send_xl(1, 0).start()
        each_y(1, lambda c: c.start())

        def y_to_x(h, n):
            k = order[n]
            recv_y(h, k).wait_recv()
            if n == 3:
                each_forward_y(h, lambda c: c.start())
            send_xr(h, k).start()
            send_xl(h, k).start()

        def pass_on(h, n):
            k = order[n]
            recv_xr(h, k).wait_recv()
            send_fr(h, k).start()
            recv_xl(h, k).wait_recv()
            send_fl(h, k).start()

        def across_row():
            recv_fr(0, 0).wait_recv()
            recv_fl(0, 0).wait_recv()
            for k in range(1, YN):
                send_yd(k).start()

        def all_in(h):
            for n in range(1, YN):
                if h == 0:
                    recv_xr(0, order[n]).wait_recv()
                    recv_xl(0, order[n]).wait_recv()
                    recv_yd(n).wait_recv()
                else:
                    recv_fr(1, order[n - 1]).wait_recv()
                    recv_fl(1, order[n - 1]).wait_recv()
            if h == 1:
                recv_xr(1, k_far).wait_recv()
                recv_xl(1, k_far).wait_recv()
                recv_x2().wait_recv()

        count_col = jnp.zeros((CAPS, 1), jnp.int32)
        row16 = lax.broadcasted_iota(jnp.int32, (CAPS, 1), 0)
        for c in range(CAPS):
            count_col = jnp.where(row16 == c, counts[c], count_col)
        inv_count = 1.0 / count_col.astype(F32)
        scale_inv = 1.0 / (float(HD) ** 0.5)
        for i in range(SUBS):
            caption = lax.broadcasted_iota(jnp.int32, (CAPS, SUB), 0)
            token = lax.broadcasted_iota(jnp.int32, (CAPS, SUB), 1) + (i * SUB)
            held = (token // L == caption) & (token % L < count_col)
            live_sc[i] = held.astype(F32)
        hid_sum = jnp.zeros((CAPS, HD), F32)
        for i in range(SUBS):
            hid_sum = hid_sum + dot_nn(live_sc[i].astype(BF16), hid[i * SUB:(i + 1) * SUB, :])
        hid_hi, hid_lo = split_two(hid_sum * inv_count)
        place = (
            lax.broadcasted_iota(jnp.int32, (HD, D), 1)
            == lax.broadcasted_iota(jnp.int32, (HD, D), 0) + mp * HD
        ).astype(F32).astype(BF16)
        share_hid[...] = dot_nn(hid_hi, place) + dot_nn(hid_lo, place)
        grad[...] = jnp.zeros_like(grad)
        outer[...] = jnp.zeros_like(outer)

        def forward_sub(h, s):
            i = h * 2 + s
            values = gat[h, :, s].astype(F32).reshape(D, SUB)
            center = jnp.sum(values, axis=0, keepdims=True) * (1.0 / D)
            values = values - center
            spread = jnp.sum(values * values, axis=0, keepdims=True) * (1.0 / D)
            normed = (values * lax.rsqrt(spread + 1e-06)).astype(BF16)
            nrm[i] = normed
            packed = dot_nn(wt[...], normed)
            q = packed[0:HD].astype(BF16)
            key = packed[HD:2 * HD].astype(BF16)
            val = packed[2 * HD:3 * HD].astype(BF16)
            qt[i] = q
            kt[i] = key
            vt[i] = val
            eye_s = eye(SUB)
            key_tok = dot_nt(eye_s, key).astype(BF16)
            vtok[i] = dot_nt(eye_s, val).astype(BF16)
            live_here = live_sc[i].astype(BF16)
            for b in range(SUB // 128):
                lanes = slice(b * 128, (b + 1) * 128)
                scores = dot_nn(key_tok[lanes], q[:, lanes]) * scale_inv
                first = (i * SUB + b * 128) // L
                s_row = lax.broadcasted_iota(jnp.int32, (128, 128), 0)
                t_col = lax.broadcasted_iota(jnp.int32, (128, 128), 1)
                limit = jnp.where(s_row < L, counts[first], counts[first + 1] + L)
                held = (s_row < limit) & (s_row // L == t_col // L)
                top = jnp.max(jnp.where(held, scores, -1e30), axis=0, keepdims=True)
                expo = jnp.where(held, jnp.exp(jnp.where(held, scores - top, 0.0)), 0.0)
                probs = expo / jnp.sum(expo, axis=0, keepdims=True)
                prob[i, b] = probs
                wl[i, :, lanes] = dot_nt(live_here[:, lanes], probs.astype(BF16))

        y_to_x(0, 1)
        pass_on(0, 0)
        y_to_x(0, 2)
        image_step(0, 2)
        pass_on(1, 0)
        image_step(1, 1)
        y_to_x(1, 1)
        across_row()
        y_to_x(0, 3)
        y_to_x(1, 2)
        image_step(0, 3)
        image_step(1, 2)
        y_to_x(1, 3)
        send_x2().start()
        pass_on(1, 1)
        pass_on(1, 2)
        all_in(0)
        forward_sub(0, 0)
        for step in range(4, last_step + 1):
            image_step(0, step)
        image_step(1, 3)
        forward_sub(0, 1)
        all_in(1)
        forward_sub(1, 0)
        forward_sub(1, 1)

        mix = jnp.zeros((CAPS, HD), F32)
        for i in range(SUBS):
            mix = mix + dot_nt(wl[i].astype(BF16), vt[i])
        mix = mix * inv_count
        mix_hi, mix_lo = split_two(mix)
        w_rows = w_out[...]
        share = dot_nn(mix_hi, w_rows) + dot_nn(mix_lo, w_rows) + share_hid[...]
        for j in range(SLICES):
            part[j] = share[:, j * 128:(j + 1) * 128]

        def send_b1(j):
            return remote(part.at[j], part_in.at[mp], b1_s.at[j], b1_r.at[mp], (dp, j))

        def recv_b1(step):
            src = (mp + step) % MP
            return remote(part_in.at[src], part_in.at[src], b1_s.at[0], b1_r.at[src], (dp, mp))

        def send_b2(step):
            own = pooled_in.at[mp]
            return remote(own, own, b2_s.at[step - 1], b2_r.at[mp], (dp, (mp + step) % MP))

        def recv_b2(j):
            return remote(pooled_in.at[j], pooled_in.at[j], b2_s.at[0], b2_r.at[j], (dp, mp))

        for j in range(SLICES):
            @pl.when(mp != j)
            def _():
                send_b1(j).start()

        for step in range(4, last_step + 1):
            image_step(1, step)

        @pl.when(mp < SLICES)
        def _():
            total = part[mp]
            for step in range(1, MP):
                recv_b1(step).wait_recv()
                total = total + part_in[(mp + step) % MP]
            pooled_in[mp] = total
            for step in range(1, MP):
                send_b2(step).start()

        for q in range(2):
            for s in range(zn):
                recv_is(q, s).wait_recv()

        for j in range(SLICES):
            @pl.when(mp != j)
            def _():
                recv_b2(j).wait_recv()

        pooled = jnp.concatenate([pooled_in[j] for j in range(SLICES)], axis=1)
        inv_norm = lax.rsqrt(jnp.sum(pooled * pooled, axis=1, keepdims=True) + 1e-06)
        text_emb = pooled * inv_norm
        pictures = img[...].reshape(zn * 4 * CAPS, D)
        logit_scale = jnp.exp(jnp.full((CAPS, 1), params[0], F32))
        logits = logit_scale * dot_nt(text_emb.astype(BF16), pictures) + params[1]
        mine = ((z * 2 + core) * 2 + yh) * CAPS
        shape = (CAPS, zn * 4 * CAPS)
        same = lax.broadcasted_iota(jnp.int32, shape, 1) == lax.broadcasted_iota(jnp.int32, shape, 0) + mine
        label = jnp.where(same, 1.0, -1.0).astype(F32)
        pair_grad = -label * jax.nn.sigmoid(-label * logits)
        text_grad = logit_scale * dot_nn(pair_grad.astype(BF16), pictures)
        along = jnp.sum(text_emb * text_grad, axis=1, keepdims=True)
        pooled_grad = (text_grad - text_emb * along) * inv_norm
        lane = lax.broadcasted_iota(jnp.int32, (HD, 3 * HD), 1)
        tile = (lane % HD == lax.broadcasted_iota(jnp.int32, (HD, 3 * HD), 0)).astype(F32).astype(BF16)
        mix_tiled = dot_nn(mix_hi, tile)
        grad_cols = dot_tn(pooled_grad.astype(BF16), eye(CAPS)).reshape(D // OWN, 3, 8, CAPS)
        lane = lax.broadcasted_iota(jnp.int32, (CAPS, 3 * HD), 1)
        total = None
        for b in range(3):
            term = dot_nn(
                grad_cols[:, b].reshape(D // 3, CAPS).astype(BF16),
                jnp.where(lane // HD == b, mix_tiled, 0.0).astype(BF16),
            )
            total = term if total is None else total + term
        outer[:, 0:3 * HD] = total
        per_caption = dot_nt(w_rows, (pooled_grad * inv_count).astype(BF16)).astype(BF16)

        grads = []
        for i in range(SUBS):
            pull = dot_nn(vtok[i], per_caption)
            owner = lax.broadcasted_iota(jnp.int32, (SUB, CAPS), 0) // L + (i * SUB // L)
            pull = jnp.sum(
                jnp.where(owner == lax.broadcasted_iota(jnp.int32, (SUB, CAPS), 1), pull, 0.0),
                axis=1, keepdims=True,
            )
            dq, dk = [], []
            for b in range(SUB // 128):
                lanes = slice(b * 128, (b + 1) * 128)
                first = (i * SUB + b * 128) // L
                t_row = lax.broadcasted_iota(jnp.int32, (1, 128), 1)
                limit = jnp.where(t_row < L, counts[first], counts[first + 1] + L)
                factor = jnp.where(t_row < limit, scale_inv, 0.0)
                probs = prob[i, b]
                here = pull[lanes]
                mean_pull = jnp.sum(probs * here, axis=0, keepdims=True)
                score_grad = (probs * (here - mean_pull) * factor).astype(BF16)
                dq.append(dot_nn(kt[i, :, lanes], score_grad))
                dk.append(dot_nt(qt[i, :, lanes], score_grad))
            dv = dot_nn(per_caption, wl[i].astype(BF16))
            qkv_grad = jnp.concatenate(
                [jnp.concatenate(dq, axis=1), jnp.concatenate(dk, axis=1), dv], axis=0
            ).astype(BF16)
            grads.append(qkv_grad)

        chips = per // 2

        def first_row(p):
            return at_z(hop(p)) * 4 + side(p) * 2

        def rows_of(p, which):
            inside = (p // 2 % chips) * (4 * OWN) + side(p) * (2 * OWN) + which * OWN
            return jnp.concatenate(
                [
                    grad[p // per, pl.ds(pl.multiple_of(inside, 8), OWN), :],
                    outer[pl.ds(pl.multiple_of((first_row(p) + which) * 8, 8), 8), :],
                ],
                axis=0,
            )

        def send_c1(g):
            return remote(
                sib_out.at[pl.ds(g * per, per)], sib_in.at[pl.ds(g * per, per)],
                c1_s.at[g], c1_r.at[g], sibling,
            )

        def send_c2(p):
            return remote(z_out.at[p], z_in.at[p], c2_s.at[p], c2_r.at[p], dev_c(p))

        def group_grad(g):
            total = None
            for i in range(SUBS):
                left = jnp.concatenate(
                    [
                        nrm[i, pl.ds(pl.multiple_of(at_z(hop(p)) * (4 * OWN), 32), 4 * OWN), :]
                        for p in range(g * per, (g + 1) * per, 2)
                    ],
                    axis=0,
                )
                term = dot_nt(left, grads[i])
                total = term if total is None else total + term
            grad[g, :, 0:3 * HD] = total
            for p in range(g * per, (g + 1) * per):
                sib_out[p] = rows_of(p, 1 - core).astype(BF16)
            send_c1(g).start()

        def group_send(g):
            send_c1(g).wait_recv()
            for p in range(g * per, (g + 1) * per):
                summed = rows_of(p, core) + sib_in[p].astype(F32)
                if p < dests - 1:
                    z_out[p] = summed.astype(BF16)
                    send_c2(p).start()
                else:
                    acc[...] = summed

        group_grad(0)
        for g in range(1, GROUPS):
            group_grad(g)
            group_send(g - 1)
        group_send(GROUPS - 1)
        total = acc[...]
        for p in range(dests - 1):
            send_c2(p).wait_recv()
            total = total + z_in[p].astype(F32)
        gq_out[...] = total[0:OWN, 0:3 * HD]
        go_out[...] = jnp.concatenate(
            [total[OWN:ROWS, b * HD:(b + 1) * HD] for b in range(3)], axis=0
        )

        for h in range(2):
            each_y(h, lambda c: c.wait_send())
            each_forward_y(h, lambda c: c.wait_send())
            for k in range(YN):
                send_xr(h, k).wait_send()
                send_xl(h, k).wait_send()
        for h, n in ((0, 0), (1, 0), (1, 1), (1, 2)):
            send_fr(h, order[n]).wait_send()
            send_fl(h, order[n]).wait_send()
        for k in range(1, YN):
            send_yd(k).wait_send()
        send_x2().wait_send()
        send_iy().wait_send()
        for q in range(2):
            for d in range(1, right_most + 1):
                send_ir(q, d).wait_send()
            for d in range(1, left_most + 1):
                send_il(q, d).wait_send()
            for s in range(zn):
                send_is(q, s).wait_send()
        for j in range(SLICES):
            @pl.when(mp != j)
            def _():
                send_b1(j).wait_send()

        @pl.when(mp < SLICES)
        def _():
            for step in range(1, MP):
                send_b2(step).wait_send()

        for g in range(GROUPS):
            send_c1(g).wait_send()
        for p in range(dests - 1):
            send_c2(p).wait_send()

    return kernel


def solution(mesh):
    zn = mesh.shape["dp"] // 4
    dma = pltpu.SemaphoreType.DMA
    right_most, left_most = zn // 2, (zn - 1) // 2
    dests = 2 * zn
    vmem = pl.BlockSpec(memory_space=pltpu.VMEM)
    smem = pl.BlockSpec(memory_space=pltpu.SMEM)

    def on_device(hidden, counts, w_qkv, w_out, images, logit_params):
        gq, go = pl.pallas_call(
            make_kernel(zn),
            out_shape=(
                jax.ShapeDtypeStruct((OWN, 3 * HD), F32),
                jax.ShapeDtypeStruct((OWN, HD), F32),
            ),
            in_specs=[vmem, smem, vmem, vmem, vmem, smem],
            out_specs=(vmem, vmem),
            scratch_shapes=[
                pltpu.VMEM((2, MP, 2, HD, SUB), BF16),
                pltpu.VMEM((SUBS, D, SUB), BF16),
                pltpu.VMEM((zn, 2, 2, CAPS, D), BF16),
                pltpu.VMEM((SUBS, HD, SUB), BF16),
                pltpu.VMEM((SUBS, HD, SUB), BF16),
                pltpu.VMEM((SUBS, HD, SUB), BF16),
                pltpu.VMEM((SUBS, SUB, HD), BF16),
                pltpu.VMEM((SUBS, SUB // 128, 128, 128), F32),
                pltpu.VMEM((SUBS, CAPS, SUB), F32),
                pltpu.VMEM((SUBS, CAPS, SUB), F32),
                pltpu.VMEM((CAPS, D), F32),
                pltpu.VMEM((SLICES, CAPS, 128), F32),
                pltpu.VMEM((MP, CAPS, 128), F32),
                pltpu.VMEM((SLICES, CAPS, 128), F32),
                pltpu.VMEM((GROUPS, D // GROUPS, WIDE), F32),
                pltpu.VMEM((D // 3, WIDE), F32),
                pltpu.VMEM((dests, ROWS, WIDE), BF16),
                pltpu.VMEM((dests, ROWS, WIDE), BF16),
                pltpu.VMEM((dests - 1, ROWS, WIDE), BF16),
                pltpu.VMEM((dests - 1, ROWS, WIDE), BF16),
                pltpu.VMEM((ROWS, WIDE), F32),
                dma((2, YN - 1)), dma((2, YN - 1)), dma((2,)),
                dma((2, YN)), dma((2, YN)), dma((2, YN)), dma((2, YN)),
                dma((2, YN)), dma((2, YN)), dma((2, YN)), dma((2, YN)),
                dma((YN - 1,)), dma((YN - 1,)), dma, dma,
                dma, dma,
                dma((2, right_most)), dma((2, right_most)), dma((2, left_most)), dma((2, left_most)),
                dma((2, zn)), dma((2, zn)),
                dma((SLICES,)), dma((MP,)), dma((MP - 1,)), dma((SLICES,)),
                dma((GROUPS,)), dma((GROUPS,)), dma((dests - 1,)), dma((dests - 1,)),
            ],
            compiler_params=pltpu.CompilerParams(
                collective_id=0, has_side_effects=True, vmem_limit_bytes=40 * 1024 * 1024
            ),
        )(hidden.reshape(CAPS * L, HD), counts, w_qkv.T, w_out, images, logit_params)
        return gq, go.T

    placed = (P("dp", None, "mp"), P("dp"), P(None, "mp"), P("mp", None), P("dp", None), P())
    return jax.shard_map(
        on_device,
        mesh=mesh,
        in_specs=placed,
        out_specs=(P("dp", "mp"), P("mp", "dp")),
        check_vma=False,
    )
```

```python
import jax
import jax.numpy as jnp
from jax import lax
from jax.experimental import pallas as pl
from jax.experimental.pallas import tpu as pltpu
from jax.sharding import PartitionSpec as P

D = 1152
HD = 72
L = 64
CAPS = 16
XN = 4
YN = 4
MP = XN * YN
SUB = 256
SUBS = CAPS * L // SUB
WIDE = 256
OWN = 24
ROWS = 32
GROUPS = 3
REACH = 3
SLICES = D // 128

MESH = pl.DeviceIdType.MESH
F32 = jnp.float32
BF16 = jnp.bfloat16


def dot_nn(a, b):
    return lax.dot_general(a, b, (((1,), (0,)), ((), ())), preferred_element_type=F32)


def dot_nt(a, b):
    return lax.dot_general(a, b, (((1,), (1,)), ((), ())), preferred_element_type=F32)


def dot_tn(a, b):
    return lax.dot_general(a, b, (((0,), (0,)), ((), ())), preferred_element_type=F32)


def eye(n):
    rows = lax.broadcasted_iota(jnp.int32, (n, n), 0)
    cols = lax.broadcasted_iota(jnp.int32, (n, n), 1)
    return (rows == cols).astype(F32).astype(BF16)


def split_two(a):
    high = a.astype(BF16)
    return high, (a - high.astype(F32)).astype(BF16)


def make_kernel(zn):
    right_most, left_most = zn // 2, (zn - 1) // 2
    dests = 2 * zn
    per = dests // GROUPS

    def kernel(
        hid, counts, wt, w_out, images, params,
        gq_out, go_out,
        gat, nrm, img, qt, kt, vt, vtok, prob, wl, live_sc, share_hid,
        part, part_in, pooled_in, grad, outer, sib_out, sib_in, z_out, z_in, acc,
        y_s, y_r, yf_s, xr_s, xr_r, xl_s, xl_r, fr_s, fr_r, fl_s, fl_r, yd_s, yd_r,
        iy_s, iy_r, ir_s, ir_r, il_s, il_r, is_s, is_r,
        b1_s, b1_r, b2_s, b2_r, c1_s, c1_r, c2_s, c2_r,
    ):
        dp, mp = lax.axis_index("dp"), lax.axis_index("mp")
        core, yh, z = dp % 2, (dp // 2) % 2, dp // 4
        x, y = mp % XN, mp // XN
        sibling = (dp + 1 - 2 * core, mp)
        across = (dp + 2 - 4 * yh, mp)

        def at_z(step):
            return (z + zn + step) % zn

        def dev_z(step):
            return (at_z(step) * 4 + yh * 2 + core, mp)

        def hop(p):
            q = p // 2
            return (zn // 2 + ((q + 1) // 2) * (1 - 2 * (q % 2)) + zn) % zn

        def side(p):
            return yh if p % 2 == 1 else 1 - yh

        def dev_c(p):
            return (at_z(hop(p)) * 4 + side(p) * 2 + core, mp)

        def slot(dx, dy):
            return ((y + YN + dy) % YN) * XN + (x + XN + dx) % XN

        def remote(src, dst, send, recv, device):
            return pltpu.make_async_remote_copy(
                src_ref=src, dst_ref=dst, send_sem=send, recv_sem=recv,
                device_id=device, device_id_type=MESH,
            )

        barrier = pltpu.get_barrier_semaphore()
        greeted = [sibling, across]
        greeted += [(dp, slot(0, k)) for k in range(1, YN)] + [(dp, slot(1, 0)), (dp, slot(-1, 0))]
        greeted += [dev_z(d) for d in (1, -1, 2, -2, 3, -3)]
        for device in greeted:
            pl.semaphore_signal(barrier, inc=1, device_id=device, device_id_type=MESH)

        eye_hd = eye(HD)
        for i in range(SUBS):
            gat[i // 2, mp, i % 2] = dot_nt(eye_hd, hid[i * SUB:(i + 1) * SUB, :]).astype(BF16)
        img[z, core, yh] = images[...].astype(BF16)

        pl.semaphore_wait(barrier, len(greeted))

        def send_y(h, k):
            own = gat.at[h, mp]
            return remote(own, own, y_s.at[h, k - 1], y_r.at[h, k - 1], (dp, slot(0, k)))

        def recv_y(h, k):
            got = gat.at[h, slot(0, -k)]
            return remote(got, got, y_s.at[h, k - 1], y_r.at[h, k - 1], (dp, slot(0, k)))

        def forward_y(h, up):
            block = gat.at[h, slot(0, -2)]
            if up:
                return remote(block, block, yf_s.at[h], y_r.at[h, 2], (dp, slot(0, 1)))
            return remote(block, block, yf_s.at[h], y_r.at[h, 0], (dp, slot(0, -1)))

        def each_y(h, act):
            @pl.when(y != 3)
            def _():
                act(send_y(h, 1))

            act(send_y(h, 2))

            @pl.when(y != 0)
            def _():
                act(send_y(h, 3))

        def each_forward_y(h, act):
            @pl.when(y == 1)
            def _():
                act(forward_y(h, False))

            @pl.when(y == 2)
            def _():
                act(forward_y(h, True))

        k_near = 3 - 2 * (y % 2)
        k_far = 1 + (y + 1) // 2
        order = (0, k_near, 6 - k_near - k_far, k_far)

        def send_xr(h, k):
            block = gat.at[h, slot(0, -k)]
            return remote(block, block, xr_s.at[h, k], xr_r.at[h, k], (dp, slot(1, 0)))

        def recv_xr(h, k):
            block = gat.at[h, slot(-1, -k)]
            return remote(block, block, xr_s.at[h, k], xr_r.at[h, k], (dp, slot(1, 0)))

        def send_xl(h, k):
            block = gat.at[h, slot(0, -k)]
            return remote(block, block, xl_s.at[h, k], xl_r.at[h, k], (dp, slot(-1, 0)))

        def recv_xl(h, k):
            block = gat.at[h, slot(1, -k)]
            return remote(block, block, xl_s.at[h, k], xl_r.at[h, k], (dp, slot(-1, 0)))

        def send_fr(h, k):
            block = gat.at[h, slot(-1, -k), 0]
            return remote(block, block, fr_s.at[h, k], fr_r.at[h, k], (dp, slot(1, 0)))

        def recv_fr(h, k):
            block = gat.at[h, slot(-2, -k), 0]
            return remote(block, block, fr_s.at[h, k], fr_r.at[h, k], (dp, slot(1, 0)))

        def send_fl(h, k):
            block = gat.at[h, slot(1, -k), 1]
            return remote(block, block, fl_s.at[h, k], fl_r.at[h, k], (dp, slot(-1, 0)))

        def recv_fl(h, k):
            block = gat.at[h, slot(2, -k), 1]
            return remote(block, block, fl_s.at[h, k], fl_r.at[h, k], (dp, slot(-1, 0)))

        def send_yd(h, k):
            block = gat.at[h, slot(2, 0)]
            return remote(block, block, yd_s.at[h, k - 1], yd_r.at[h, k - 1], (dp, slot(0, k)))

        def recv_yd(h, k):
            block = gat.at[h, slot(2, -k)]
            return remote(block, block, yd_s.at[h, k - 1], yd_r.at[h, k - 1], (dp, slot(0, k)))

        def line(q):
            return yh if q == 0 else 1 - yh

        def send_iy():
            own = img.at[z, core, yh]
            return remote(own, own, iy_s, iy_r, across)

        def recv_iy():
            got = img.at[z, core, 1 - yh]
            return remote(got, got, iy_s, iy_r, across)

        def send_ir(q, d):
            reach = (d - 1) % REACH + 1
            block = img.at[at_z(reach - d), core, line(q)]
            return remote(block, block, ir_s.at[q, d - 1], ir_r.at[q, d - 1], dev_z(reach))

        def recv_ir(q, d):
            block = img.at[at_z(-d), core, line(q)]
            return remote(block, block, ir_s.at[q, d - 1], ir_r.at[q, d - 1], dev_z(1))

        def send_il(q, d):
            reach = (d - 1) % REACH + 1
            block = img.at[at_z(d - reach), core, line(q)]
            return remote(block, block, il_s.at[q, d - 1], il_r.at[q, d - 1], dev_z(-reach))

        def recv_il(q, d):
            block = img.at[at_z(d), core, line(q)]
            return remote(block, block, il_s.at[q, d - 1], il_r.at[q, d - 1], dev_z(-1))

        def send_is(q, s):
            block = img.at[at_z(s), core, line(q)]
            n = (s + zn) % zn
            return remote(block, block, is_s.at[q, n], is_r.at[q, n], sibling)

        def recv_is(q, s):
            block = img.at[at_z(s), 1 - core, line(q)]
            n = (s + zn) % zn
            return remote(block, block, is_s.at[q, n], is_r.at[q, n], sibling)

        def reach_out(q, first):
            for d in range(first + REACH - 1, first - 1, -1):
                if d <= right_most:
                    send_ir(q, d).start()
                if d <= left_most:
                    send_il(q, d).start()

        def image_step(q, step):
            if step == 1:
                if q == 1:
                    recv_iy().wait_recv()
                reach_out(q, 1)
                send_is(q, 0).start()
                return
            far = (step - 1) * REACH
            for d in range(far, far - REACH, -1):
                if d <= right_most:
                    recv_ir(q, d).wait_recv()
                if d <= left_most:
                    recv_il(q, d).wait_recv()
                if d == far:
                    reach_out(q, d + 1)
            for d in range(far - REACH + 1, far + 1):
                if d <= right_most:
                    send_is(q, -d).start()
                if d <= left_most:
                    send_is(q, d).start()

        last_step = (right_most + REACH - 1) // REACH + 1

        each_y(0, lambda c: c.start())
        send_xr(0, 0).start()
        send_xl(0, 0).start()
        send_iy().start()
        image_step(0, 1)
        send_xr(1, 0).start()
        send_xl(1, 0).start()
        each_y(1, lambda c: c.start())

        def y_to_x(h, n):
            k = order[n]
            recv_y(h, k).wait_recv()
            if n == 3:
                each_forward_y(h, lambda c: c.start())
            send_xr(h, k).start()
            send_xl(h, k).start()

        def pass_on(h, n):
            k = order[n]
            recv_xr(h, k).wait_recv()
            send_fr(h, k).start()
            recv_xl(h, k).wait_recv()
            send_fl(h, k).start()

        def across_row(h):
            recv_fr(h, 0).wait_recv()
            recv_fl(h, 0).wait_recv()
            for k in range(1, YN):
                send_yd(h, k).start()

        def all_in(h):
            for n in range(1, YN):
                recv_xr(h, order[n]).wait_recv()
                recv_xl(h, order[n]).wait_recv()
                recv_yd(h, n).wait_recv()

        count_col = jnp.zeros((CAPS, 1), jnp.int32)
        row16 = lax.broadcasted_iota(jnp.int32, (CAPS, 1), 0)
        for c in range(CAPS):
            count_col = jnp.where(row16 == c, counts[c], count_col)
        inv_count = 1.0 / count_col.astype(F32)
        scale_inv = 1.0 / (float(HD) ** 0.5)
        for i in range(SUBS):
            caption = lax.broadcasted_iota(jnp.int32, (CAPS, SUB), 0)
            token = lax.broadcasted_iota(jnp.int32, (CAPS, SUB), 1) + (i * SUB)
            held = (token // L == caption) & (token % L < count_col)
            live_sc[i] = held.astype(F32)
        hid_sum = jnp.zeros((CAPS, HD), F32)
        for i in range(SUBS):
            hid_sum = hid_sum + dot_nn(live_sc[i].astype(BF16), hid[i * SUB:(i + 1) * SUB, :])
        hid_hi, hid_lo = split_two(hid_sum * inv_count)
        place = (
            lax.broadcasted_iota(jnp.int32, (HD, D), 1)
            == lax.broadcasted_iota(jnp.int32, (HD, D), 0) + mp * HD
        ).astype(F32).astype(BF16)
        share_hid[...] = dot_nn(hid_hi, place) + dot_nn(hid_lo, place)
        grad[...] = jnp.zeros_like(grad)
        outer[...] = jnp.zeros_like(outer)

        def forward_sub(h, s):
            i = h * 2 + s
            values = gat[h, :, s].astype(F32).reshape(D, SUB)
            center = jnp.sum(values, axis=0, keepdims=True) * (1.0 / D)
            values = values - center
            spread = jnp.sum(values * values, axis=0, keepdims=True) * (1.0 / D)
            normed = (values * lax.rsqrt(spread + 1e-06)).astype(BF16)
            nrm[i] = normed
            packed = dot_nn(wt[...], normed)
            q = packed[0:HD].astype(BF16)
            key = packed[HD:2 * HD].astype(BF16)
            val = packed[2 * HD:3 * HD].astype(BF16)
            qt[i] = q
            kt[i] = key
            vt[i] = val
            eye_s = eye(SUB)
            key_tok = dot_nt(eye_s, key).astype(BF16)
            vtok[i] = dot_nt(eye_s, val).astype(BF16)
            live_here = live_sc[i].astype(BF16)
            for b in range(SUB // 128):
                lanes = slice(b * 128, (b + 1) * 128)
                scores = dot_nn(key_tok[lanes], q[:, lanes]) * scale_inv
                first = (i * SUB + b * 128) // L
                s_row = lax.broadcasted_iota(jnp.int32, (128, 128), 0)
                t_col = lax.broadcasted_iota(jnp.int32, (128, 128), 1)
                limit = jnp.where(s_row < L, counts[first], counts[first + 1] + L)
                held = (s_row < limit) & (s_row // L == t_col // L)
                top = jnp.max(jnp.where(held, scores, -1e30), axis=0, keepdims=True)
                expo = jnp.where(held, jnp.exp(jnp.where(held, scores - top, 0.0)), 0.0)
                probs = expo / jnp.sum(expo, axis=0, keepdims=True)
                prob[i, b] = probs
                wl[i, :, lanes] = dot_nt(live_here[:, lanes], probs.astype(BF16))

        y_to_x(0, 1)
        pass_on(0, 0)
        y_to_x(0, 2)
        pass_on(1, 0)
        image_step(1, 1)
        y_to_x(1, 1)
        across_row(0)
        y_to_x(0, 3)
        across_row(1)
        y_to_x(1, 2)
        image_step(0, 2)
        y_to_x(1, 3)
        image_step(1, 2)
        all_in(0)
        forward_sub(0, 0)
        forward_sub(0, 1)
        all_in(1)
        forward_sub(1, 0)
        forward_sub(1, 1)

        mix = jnp.zeros((CAPS, HD), F32)
        for i in range(SUBS):
            mix = mix + dot_nt(wl[i].astype(BF16), vt[i])
        mix = mix * inv_count
        mix_hi, mix_lo = split_two(mix)
        w_rows = w_out[...]
        share = dot_nn(mix_hi, w_rows) + dot_nn(mix_lo, w_rows) + share_hid[...]
        for j in range(SLICES):
            part[j] = share[:, j * 128:(j + 1) * 128]

        def send_b1(j):
            return remote(part.at[j], part_in.at[mp], b1_s.at[j], b1_r.at[mp], (dp, j))

        def recv_b1(step):
            src = (mp + step) % MP
            return remote(part_in.at[src], part_in.at[src], b1_s.at[0], b1_r.at[src], (dp, mp))

        def send_b2(step):
            own = pooled_in.at[mp]
            return remote(own, own, b2_s.at[step - 1], b2_r.at[mp], (dp, (mp + step) % MP))

        def recv_b2(j):
            return remote(pooled_in.at[j], pooled_in.at[j], b2_s.at[0], b2_r.at[j], (dp, mp))

        for j in range(SLICES):
            @pl.when(mp != j)
            def _():
                send_b1(j).start()

        @pl.when(mp < SLICES)
        def _():
            total = part[mp]
            for step in range(1, MP):
                recv_b1(step).wait_recv()
                total = total + part_in[(mp + step) % MP]
            pooled_in[mp] = total
            for step in range(1, MP):
                send_b2(step).start()

        for step in range(3, last_step + 1):
            for q in range(2):
                image_step(q, step)
        for q in range(2):
            for s in range(zn):
                recv_is(q, s).wait_recv()

        for j in range(SLICES):
            @pl.when(mp != j)
            def _():
                recv_b2(j).wait_recv()

        pooled = jnp.concatenate([pooled_in[j] for j in range(SLICES)], axis=1)
        inv_norm = lax.rsqrt(jnp.sum(pooled * pooled, axis=1, keepdims=True) + 1e-06)
        text_emb = pooled * inv_norm
        pictures = img[...].reshape(zn * 4 * CAPS, D)
        logit_scale = jnp.exp(jnp.full((CAPS, 1), params[0], F32))
        logits = logit_scale * dot_nt(text_emb.astype(BF16), pictures) + params[1]
        mine = ((z * 2 + core) * 2 + yh) * CAPS
        shape = (CAPS, zn * 4 * CAPS)
        same = lax.broadcasted_iota(jnp.int32, shape, 1) == lax.broadcasted_iota(jnp.int32, shape, 0) + mine
        label = jnp.where(same, 1.0, -1.0).astype(F32)
        pair_grad = -label * jax.nn.sigmoid(-label * logits)
        text_grad = logit_scale * dot_nn(pair_grad.astype(BF16), pictures)
        along = jnp.sum(text_emb * text_grad, axis=1, keepdims=True)
        pooled_grad = (text_grad - text_emb * along) * inv_norm
        lane = lax.broadcasted_iota(jnp.int32, (HD, 3 * HD), 1)
        tile = (lane % HD == lax.broadcasted_iota(jnp.int32, (HD, 3 * HD), 0)).astype(F32).astype(BF16)
        mix_tiled = dot_nn(mix_hi, tile)
        grad_cols = dot_tn(pooled_grad.astype(BF16), eye(CAPS)).reshape(D // OWN, 3, 8, CAPS)
        lane = lax.broadcasted_iota(jnp.int32, (CAPS, 3 * HD), 1)
        total = None
        for b in range(3):
            term = dot_nn(
                grad_cols[:, b].reshape(D // 3, CAPS).astype(BF16),
                jnp.where(lane // HD == b, mix_tiled, 0.0).astype(BF16),
            )
            total = term if total is None else total + term
        outer[:, 0:3 * HD] = total
        per_caption = dot_nt(w_rows, (pooled_grad * inv_count).astype(BF16)).astype(BF16)

        grads = []
        for i in range(SUBS):
            pull = dot_nn(vtok[i], per_caption)
            owner = lax.broadcasted_iota(jnp.int32, (SUB, CAPS), 0) // L + (i * SUB // L)
            pull = jnp.sum(
                jnp.where(owner == lax.broadcasted_iota(jnp.int32, (SUB, CAPS), 1), pull, 0.0),
                axis=1, keepdims=True,
            )
            dq, dk = [], []
            for b in range(SUB // 128):
                lanes = slice(b * 128, (b + 1) * 128)
                first = (i * SUB + b * 128) // L
                t_row = lax.broadcasted_iota(jnp.int32, (1, 128), 1)
                limit = jnp.where(t_row < L, counts[first], counts[first + 1] + L)
                factor = jnp.where(t_row < limit, scale_inv, 0.0)
                probs = prob[i, b]
                here = pull[lanes]
                mean_pull = jnp.sum(probs * here, axis=0, keepdims=True)
                score_grad = (probs * (here - mean_pull) * factor).astype(BF16)
                dq.append(dot_nn(kt[i, :, lanes], score_grad))
                dk.append(dot_nt(qt[i, :, lanes], score_grad))
            dv = dot_nn(per_caption, wl[i].astype(BF16))
            qkv_grad = jnp.concatenate(
                [jnp.concatenate(dq, axis=1), jnp.concatenate(dk, axis=1), dv], axis=0
            ).astype(BF16)
            grads.append(qkv_grad)

        chips = per // 2

        def first_row(p):
            return at_z(hop(p)) * 4 + side(p) * 2

        def rows_of(p, which):
            inside = (p // 2 % chips) * (4 * OWN) + side(p) * (2 * OWN) + which * OWN
            return jnp.concatenate(
                [
                    grad[p // per, pl.ds(pl.multiple_of(inside, 8), OWN), :],
                    outer[pl.ds(pl.multiple_of((first_row(p) + which) * 8, 8), 8), :],
                ],
                axis=0,
            )

        def send_c1(g):
            return remote(
                sib_out.at[pl.ds(g * per, per)], sib_in.at[pl.ds(g * per, per)],
                c1_s.at[g], c1_r.at[g], sibling,
            )

        def send_c2(p):
            return remote(z_out.at[p], z_in.at[p], c2_s.at[p], c2_r.at[p], dev_c(p))

        def group_grad(g):
            total = None
            for i in range(SUBS):
                left = jnp.concatenate(
                    [
                        nrm[i, pl.ds(pl.multiple_of(at_z(hop(p)) * (4 * OWN), 32), 4 * OWN), :]
                        for p in range(g * per, (g + 1) * per, 2)
                    ],
                    axis=0,
                )
                term = dot_nt(left, grads[i])
                total = term if total is None else total + term
            grad[g, :, 0:3 * HD] = total
            for p in range(g * per, (g + 1) * per):
                sib_out[p] = rows_of(p, 1 - core).astype(BF16)
            send_c1(g).start()

        def group_send(g):
            send_c1(g).wait_recv()
            for p in range(g * per, (g + 1) * per):
                summed = rows_of(p, core) + sib_in[p].astype(F32)
                if p < dests - 1:
                    z_out[p] = summed.astype(BF16)
                    send_c2(p).start()
                else:
                    acc[...] = summed

        group_grad(0)
        for g in range(1, GROUPS):
            group_grad(g)
            group_send(g - 1)
        group_send(GROUPS - 1)
        total = acc[...]
        for p in range(dests - 1):
            send_c2(p).wait_recv()
            total = total + z_in[p].astype(F32)
        gq_out[...] = total[0:OWN, 0:3 * HD]
        go_out[...] = jnp.concatenate(
            [total[OWN:ROWS, b * HD:(b + 1) * HD] for b in range(3)], axis=0
        )

        for h in range(2):
            each_y(h, lambda c: c.wait_send())
            each_forward_y(h, lambda c: c.wait_send())
            for k in range(YN):
                send_xr(h, k).wait_send()
                send_xl(h, k).wait_send()
            send_fr(h, 0).wait_send()
            send_fl(h, 0).wait_send()
            for k in range(1, YN):
                send_yd(h, k).wait_send()
        send_iy().wait_send()
        for q in range(2):
            for d in range(1, right_most + 1):
                send_ir(q, d).wait_send()
            for d in range(1, left_most + 1):
                send_il(q, d).wait_send()
            for s in range(zn):
                send_is(q, s).wait_send()
        for j in range(SLICES):
            @pl.when(mp != j)
            def _():
                send_b1(j).wait_send()

        @pl.when(mp < SLICES)
        def _():
            for step in range(1, MP):
                send_b2(step).wait_send()

        for g in range(GROUPS):
            send_c1(g).wait_send()
        for p in range(dests - 1):
            send_c2(p).wait_send()

    return kernel


def solution(mesh):
    zn = mesh.shape["dp"] // 4
    dma = pltpu.SemaphoreType.DMA
    right_most, left_most = zn // 2, (zn - 1) // 2
    dests = 2 * zn
    vmem = pl.BlockSpec(memory_space=pltpu.VMEM)
    smem = pl.BlockSpec(memory_space=pltpu.SMEM)

    def on_device(hidden, counts, w_qkv, w_out, images, logit_params):
        gq, go = pl.pallas_call(
            make_kernel(zn),
            out_shape=(
                jax.ShapeDtypeStruct((OWN, 3 * HD), F32),
                jax.ShapeDtypeStruct((OWN, HD), F32),
            ),
            in_specs=[vmem, smem, vmem, vmem, vmem, smem],
            out_specs=(vmem, vmem),
            scratch_shapes=[
                pltpu.VMEM((2, MP, 2, HD, SUB), BF16),
                pltpu.VMEM((SUBS, D, SUB), BF16),
                pltpu.VMEM((zn, 2, 2, CAPS, D), BF16),
                pltpu.VMEM((SUBS, HD, SUB), BF16),
                pltpu.VMEM((SUBS, HD, SUB), BF16),
                pltpu.VMEM((SUBS, HD, SUB), BF16),
                pltpu.VMEM((SUBS, SUB, HD), BF16),
                pltpu.VMEM((SUBS, SUB // 128, 128, 128), F32),
                pltpu.VMEM((SUBS, CAPS, SUB), F32),
                pltpu.VMEM((SUBS, CAPS, SUB), F32),
                pltpu.VMEM((CAPS, D), F32),
                pltpu.VMEM((SLICES, CAPS, 128), F32),
                pltpu.VMEM((MP, CAPS, 128), F32),
                pltpu.VMEM((SLICES, CAPS, 128), F32),
                pltpu.VMEM((GROUPS, D // GROUPS, WIDE), F32),
                pltpu.VMEM((D // 3, WIDE), F32),
                pltpu.VMEM((dests, ROWS, WIDE), BF16),
                pltpu.VMEM((dests, ROWS, WIDE), BF16),
                pltpu.VMEM((dests - 1, ROWS, WIDE), BF16),
                pltpu.VMEM((dests - 1, ROWS, WIDE), BF16),
                pltpu.VMEM((ROWS, WIDE), F32),
                dma((2, YN - 1)), dma((2, YN - 1)), dma((2,)),
                dma((2, YN)), dma((2, YN)), dma((2, YN)), dma((2, YN)),
                dma((2, YN)), dma((2, YN)), dma((2, YN)), dma((2, YN)),
                dma((2, YN - 1)), dma((2, YN - 1)),
                dma, dma,
                dma((2, right_most)), dma((2, right_most)), dma((2, left_most)), dma((2, left_most)),
                dma((2, zn)), dma((2, zn)),
                dma((SLICES,)), dma((MP,)), dma((MP - 1,)), dma((SLICES,)),
                dma((GROUPS,)), dma((GROUPS,)), dma((dests - 1,)), dma((dests - 1,)),
            ],
            compiler_params=pltpu.CompilerParams(
                collective_id=0, has_side_effects=True, vmem_limit_bytes=40 * 1024 * 1024
            ),
        )(hidden.reshape(CAPS * L, HD), counts, w_qkv.T, w_out, images, logit_params)
        return gq, go.T

    placed = (P("dp", None, "mp"), P("dp"), P(None, "mp"), P("mp", None), P("dp", None), P())
    return jax.shard_map(
        on_device,
        mesh=mesh,
        in_specs=placed,
        out_specs=(P("dp", "mp"), P("mp", "dp")),
        check_vma=False,
    )
```
